256 devices in a mesh: dp: 2 (over y_hi), row: 8 (over z), col: 16 (over x, y_lo, core).
Axes of the slice: x: 4, y: 4 (y_hi: 2, y_lo: 2; y = y_hi * 2 + y_lo), z: 8, core: 2. Of those that a mesh axis runs over, the one named last changes fastest.
Arguments:
- partials: float32 [2, 8192, 28672], P('dp', ('row', 'col')), may hold values from -22.5 to 22.5
- clip_ratio: float32 [1], replicated, may hold values from 0.5 to 1
- start_block: float32 [28672, 128], P(('dp', 'col')), may hold values from -1 to 1
Outputs:
- update: float32 [8192, 28672], P(('row', 'col'), 'dp')
- basis: float32 [28672, 128], P(('dp', 'col'))
The draws below stay inside these ranges and needn't reach their ends.
All inputs are finite; a program needn't handle non-finite values.
Results may differ from the reference program's by a relative error of at most 0.0002.
Values sent between devices are 32-bit elements; how exact they have to be, the bound alone decides.
A program may use at most 128 MiB of HBM per device.

```python
import math
import jax
import jax.numpy as jnp
from jax import lax

M = 8192
N = 28672
K = 128
ITERS = 3
N_DP = 2


def draw_partials(key, part):
    key = jax.random.fold_in(key, 11)
    key_rows, key_cols, key_noise = jax.random.split(key, 3)
    rows = jnp.exp(jax.random.uniform(key_rows, (1, M, 1), jnp.float32, math.log(0.3), math.log(3.0)))
    cols = jnp.exp(jax.random.uniform(key_cols, (1, 1, N), jnp.float32, math.log(0.3), math.log(3.0)))
    values = jnp.clip(jax.random.normal(key_noise, (N_DP, M, N), jnp.float32), -5.0, 5.0)
    return (0.5 * values * rows * cols).astype(jnp.float32)


def levels(rng, dims, pieces, smallest, largest):
    factor_of = 1.0
    for position, blocks in pieces:
        draws = jax.random.uniform(jax.random.fold_in(jax.random.fold_in(rng, 6), position), (blocks,), jnp.float32, smallest / len(pieces), largest / len(pieces))
        factor_of = factor_of * jnp.repeat(jnp.exp(draws), dims[position] // blocks).reshape((-1,) + (1,) * (len(dims) - 1 - position))
    return factor_of


def setup_inputs(seed: int = 0) -> dict:
    seeds = jax.random.split(jax.random.key(seed), 4)
    return {
        "partials": draw_partials(jax.random.fold_in(seeds[3], 71), 0),
        "clip_ratio": jnp.clip(jax.random.uniform(seeds[1], (1,), jnp.float32, 0.5, 1.0), 0.5, 1.0),
        "start_block": jnp.clip(jax.random.uniform(seeds[2], (N, K), jnp.float32, -1.0, 1.0) * levels(seeds[2], (N, K), ((0, 32),), -0.4, 0.0), -1.0, 1.0),
    }


def orthonormal(block, gram):
    factor = jnp.linalg.cholesky(gram)
    return jax.scipy.linalg.solve_triangular(factor, block.T, lower=True).T

def reference(partials, clip_ratio, start_block):
    highest = lax.Precision.HIGHEST
    grad = lax.optimization_barrier(jnp.sum(partials, axis=0))
    vectors = start_block * math.sqrt(3.0 / N)
    second = jnp.zeros((K, K), jnp.float32)
    for step in range(ITERS):
        left = jnp.dot(grad.astype(jnp.float32), vectors.astype(jnp.float32), precision=highest, preferred_element_type=jnp.float32)
        gram = jnp.dot(left.T.astype(jnp.float32), left.astype(jnp.float32), precision=highest, preferred_element_type=jnp.float32)
        basis_left = orthonormal(left, gram)
        right = lax.dot_general(grad.astype(jnp.float32), basis_left.astype(jnp.float32), (((0,), (0,)), ((), ())), precision=highest, preferred_element_type=jnp.float32)
        second = jnp.dot(right.T.astype(jnp.float32), right.astype(jnp.float32), precision=highest, preferred_element_type=jnp.float32)
        vectors = orthonormal(right, second)
    sigma = jnp.sqrt(jnp.sqrt(jnp.sum(second * second)))
    limit = clip_ratio[0] * (math.sqrt(M) + math.sqrt(N))
    scale = limit / sigma
    return (grad * scale, vectors)
```

```python
import math

import jax
import jax.numpy as jnp
from jax import lax
from jax.experimental import pallas as pl
from jax.experimental.pallas import tpu as pltpu
from jax.sharding import PartitionSpec as P

M = 8192
N = 28672
K = 128
ITERS = 3
TR = 1024
TC = 896
ZB = 112
MESH = pl.DeviceIdType.MESH
BF = jnp.bfloat16
F32 = jnp.float32

G2_CORE, G2_X, G2_Y, G2_XG, G2_CG = 0, 1, 5, 9, 13
L_CORE, L_X, L_Y, L_XG, L_CG = 14, 15, 19, 23, 27
G1_RS, G1_AG, W_RS, W_AG = 28, 36, 44, 52
SEMS = 60


def split2(a):
    hi = a.astype(BF)
    return hi, (a - hi.astype(F32)).astype(BF)


def dot_f32(a, b, dims):
    return lax.dot_general(a, b, (dims, ((), ())), preferred_element_type=F32)


def wide(a):
    hi, lo = split2(a)
    return jnp.concatenate([hi, lo], axis=1)


def full_dot(a, b, dims):
    return lax.dot_general(
        a, b, (dims, ((), ())), precision=lax.Precision.HIGHEST, preferred_element_type=F32
    )


def split_product(hi, lo, both):
    first = jnp.dot(hi, both, preferred_element_type=F32)
    return first[:, :K] + first[:, K:] + jnp.dot(lo, both[:, :K], preferred_element_type=F32)


def inverse_factor(gram):
    lane = lax.broadcasted_iota(jnp.int32, (8, K), 1)
    sub = lax.broadcasted_iota(jnp.int32, (8, K), 0)
    col = lax.broadcasted_iota(jnp.int32, (K, K), 1)
    row = lax.broadcasted_iota(jnp.int32, (K, K), 0)

    def step(k, x):
        p = x[0:8, :]
        q = jnp.where(lane == sub, 1.0, 0.0).astype(F32)
        for j in range(8):
            piv = p[j : j + 1, j : j + 1]
            rs = lax.rsqrt(piv)
            rs = rs * (1.5 - 0.5 * piv * rs * rs)
            urow = p[j : j + 1, :] * rs
            qrow = q[j : j + 1, :] * rs
            m = jnp.where(sub > j, p[:, j : j + 1] * rs, 0.0)
            p = jnp.where(sub == j, urow, p - m * urow)
            q = jnp.where(sub == j, qrow, q - m * qrow)
        y = jnp.where(lane < 8, q, p)
        left = jnp.where((lane >= 8) & (lane < K - 8 * k), p, 0.0)

        def split3(a):
            hi = a.astype(BF).astype(F32)
            mid = (a - hi).astype(BF).astype(F32)
            return hi, mid, a - hi - mid

        lh, lm, ll = split3(left)
        yh, ym, yl = split3(y)
        a = jnp.concatenate([lh, lh, lm, lh, ll, lm], axis=0).astype(BF)
        b = jnp.concatenate([yh, ym, yh, yl, yh, ym], axis=0).astype(BF)
        upd = dot_f32(a, b, ((0,), (0,)))
        new = jnp.where(col < 8, 0.0, x) - upd
        new = jnp.where(row < K - 8 * k, new, x)
        return pltpu.roll(jnp.concatenate([new[8:, :], y], axis=0), K - 8, axis=1)

    x = lax.fori_loop(0, K // 8, step, gram)
    return jnp.where(col <= row, x, 0.0)


def kernel(
    tile,
    start,
    basis_out,
    second_out,
    thi,
    tlo,
    thit,
    tlot,
    right,
    rwide,
    left,
    lpart,
    lcore,
    lx,
    ly,
    lsum,
    wpart,
    wz,
    gram1,
    g1z,
    g1share,
    gram2,
    g2core,
    g2x,
    g2y,
    g2sum,
    factor,
    send,
    recv,
):
    d = lax.axis_index("dp")
    z = lax.axis_index("row")
    c = lax.axis_index("col")
    co = lax.rem(c, 2)
    yl = lax.rem(lax.div(c, 2), 2)
    x = lax.div(c, 4)
    y = d * 2 + yl

    def dev_core():
        return (d, z, c + 1 - 2 * co)

    def dev_x(i):
        return (d, z, i * 4 + yl * 2 + co)

    def dev_y(i):
        return (lax.div(i, 2), z, x * 4 + lax.rem(i, 2) * 2 + co)

    def dev_z(i):
        return (d, i, c)

    barrier = pltpu.get_barrier_semaphore()
    peers = [dev_core()]
    peers += [dev_x(lax.rem(x + o, 4)) for o in (1, 3, 2)]
    peers += [dev_y(lax.rem(y + o, 4)) for o in (1, 3, 2)]
    peers += [dev_z(lax.rem(z + o, 8)) for o in (1, 7, 2, 6, 3, 5, 4)]
    for dev in peers:
        pl.semaphore_signal(barrier, inc=1, device_id=dev, device_id_type=MESH)

    for i in range(TR // 128):
        part = tile[i * 128 : (i + 1) * 128, :]
        hi, lo = split2(part)
        thi[i * 128 : (i + 1) * 128, :] = hi
        tlo[i * 128 : (i + 1) * 128, :] = lo
        hi, lo = split2(part.T)
        thit[:, i * 128 : (i + 1) * 128] = hi
        tlot[:, i * 128 : (i + 1) * 128] = lo
    right[...] = start[...] * math.sqrt(3.0 / N)
    rwide[...] = wide(right[...])
    pl.semaphore_wait(barrier, len(peers))

    def copy(src, dst, it, slot_out, slot_in, dev):
        return pltpu.make_async_remote_copy(
            src_ref=src,
            dst_ref=dst,
            send_sem=send.at[it, slot_out],
            recv_sem=recv.at[it, slot_in],
            device_id=dev,
            device_id_type=MESH,
        )

    def ring(n, me, dev, base, it, src, dst):
        for o in sorted(range(1, n), key=lambda o: min(o, n - o)):
            i = lax.rem(me + o, n)
            copy(src(i), dst(me), it, base + o, base + o, dev(i)).start()

    def ring_wait(n, me, dev, base, it, src, dst):
        for o in sorted(range(1, n), key=lambda o: min(o, n - o)):
            i = lax.rem(me + n - o, n)
            copy(src(i), dst(i), it, base + o, base + o, dev(i)).wait()

    def blocks(ref, size):
        return lambda i: ref.at[pl.ds(pl.multiple_of(i * size, size), size), :]

    class Plane:
        def __init__(self, it, rows, part, core_buf, x_buf, y_buf, total, sems):
            self.it, self.rows = it, rows
            self.part, self.core_buf, self.x_buf, self.y_buf, self.total = part, core_buf, x_buf, y_buf, total
            self.s_core, self.s_x, self.s_y, self.s_xg, self.s_cg = sems
            self.half, self.unit = rows // 2, rows // 8

        def mine(self):
            return pl.ds(pl.multiple_of(co * self.half + x * self.unit, self.unit), self.unit)

        def core_copy(self):
            there = pl.ds(pl.multiple_of((1 - co) * self.half, self.half), self.half)
            return copy(self.part.at[there, :], self.core_buf.at[self.it], self.it, self.s_core, self.s_core, dev_core())

        def core_done(self):
            self.core_copy().wait()
            here = pl.ds(pl.multiple_of(co * self.half, self.half), self.half)
            self.core_buf[self.it] = self.core_buf[self.it] + self.part[here, :]

        def x_args(self):
            src = lambda i: self.core_buf.at[self.it, pl.ds(pl.multiple_of(i * self.unit, self.unit), self.unit), :]
            return (4, x, dev_x, self.s_x, self.it, src, lambda i: self.x_buf.at[self.it, i])

        def x_send(self):
            own = self.core_buf[self.it, pl.ds(pl.multiple_of(x * self.unit, self.unit), self.unit), :]
            self.x_buf[self.it, x] = own
            ring(*self.x_args())

        def x_done(self):
            ring_wait(*self.x_args())
            self.y_buf[self.it, y] = (self.x_buf[self.it, 0] + self.x_buf[self.it, 1]) + (
                self.x_buf[self.it, 2] + self.x_buf[self.it, 3]
            )

        def y_args(self):
            return (
                4,
                y,
                dev_y,
                self.s_y,
                self.it,
                lambda i: self.y_buf.at[self.it, y],
                lambda i: self.y_buf.at[self.it, i],
            )

        def y_send(self):
            ring(*self.y_args())

        def y_done(self):
            ring_wait(*self.y_args())
            self.total[self.mine(), :] = (self.y_buf[self.it, 0] + self.y_buf[self.it, 1]) + (
                self.y_buf[self.it, 2] + self.y_buf[self.it, 3]
            )

        def xg_args(self):
            place = lambda i: self.total.at[pl.ds(pl.multiple_of(co * self.half + i * self.unit, self.unit), self.unit), :]
            return (4, x, dev_x, self.s_xg, self.it, lambda i: place(x), place)

        def xg_send(self):
            ring(*self.xg_args())

        def xg_done(self):
            ring_wait(*self.xg_args())

        def cg_copy(self):
            here = self.total.at[pl.ds(pl.multiple_of(co * self.half, self.half), self.half), :]
            return copy(here, here, self.it, self.s_cg, self.s_cg, dev_core())

    def left_plane(it):
        return Plane(it, TR, lpart, lcore, lx, ly, lsum, (L_CORE, L_X, L_Y, L_XG, L_CG))

    def second_plane(it):
        return Plane(it, K, gram2, g2core, g2x, g2y, g2sum, (G2_CORE, G2_X, G2_Y, G2_XG, G2_CG))

    def iteration(it, carry):
        lp, sp = left_plane(it), second_plane(it)

        @pl.when(it > 0)
        def _():
            gram2[...] = full_dot(right[...], right[...], ((0,), (0,)))
            sp.core_copy().start()

        lpart[...] = split_product(thi[...], tlo[...], rwide[...])
        lp.core_copy().start()

        @pl.when(it > 0)
        def _():
            sp.core_done()
            sp.x_send()

        lp.core_done()
        lp.x_send()

        @pl.when(it > 0)
        def _():
            sp.x_done()
            sp.y_send()

        lp.x_done()
        lp.y_send()

        @pl.when(it > 0)
        def _():
            sp.y_done()
            sp.xg_send()

        lp.y_done()
        lp.xg_send()

        @pl.when(it > 0)
        def _():
            sp.xg_done()
            sp.cg_copy().start()

        lp.xg_done()
        lp.cg_copy().start()

        @pl.when(it > 0)
        def _():
            sp.cg_copy().wait()
            factor[...] = inverse_factor(g2sum[...])

        lp.cg_copy().wait()

        @pl.when(it == 0)
        def _():
            left[...] = lsum[...]

        @pl.when(it > 0)
        def _():
            left[...] = full_dot(lsum[...], factor[...], ((1,), (1,)))

        gram1[...] = full_dot(left[...], left[...], ((0,), (0,)))
        g1_rs = (8, z, dev_z, G1_RS, it, blocks(gram1, 16), lambda i: g1z.at[it, i])
        g1z[it, z] = gram1[pl.ds(pl.multiple_of(z * 16, 16), 16), :]
        ring(*g1_rs)

        lwide = wide(left[...])
        wpart[...] = split_product(thit[...], tlot[...], lwide)
        w_rs = (8, z, dev_z, W_RS, it, blocks(wpart, ZB), lambda i: wz.at[it, i])
        wz[it, z] = wpart[pl.ds(pl.multiple_of(z * ZB, 16), ZB), :]
        ring(*w_rs)

        ring_wait(*g1_rs)
        total = g1z[it, 0]
        for i in range(1, 8):
            total = total + g1z[it, i]
        g1share[pl.ds(pl.multiple_of(z * 16, 16), 16), :] = total
        share = blocks(g1share, 16)
        g1_ag = (8, z, dev_z, G1_AG, it, lambda i: share(z), share)
        ring(*g1_ag)

        ring_wait(*w_rs)
        total = wz[it, 0]
        for i in range(1, 8):
            total = total + wz[it, i]
        right[pl.ds(pl.multiple_of(z * ZB, 16), ZB), :] = total
        place = blocks(right, ZB)
        w_ag = (8, z, dev_z, W_AG, it, lambda i: place(z), place)
        ring(*w_ag)

        ring_wait(*g1_ag)
        factor[...] = inverse_factor(g1share[...])
        ring_wait(*w_ag)
        right[...] = full_dot(right[...], factor[...], ((1,), (1,)))
        rwide[...] = wide(right[...])
        return carry

    lax.fori_loop(0, ITERS, iteration, 0)

    sp = second_plane(ITERS)
    gram2[...] = full_dot(right[...], right[...], ((0,), (0,)))
    sp.core_copy().start()
    sp.core_done()
    sp.x_send()
    sp.x_done()
    sp.y_send()
    sp.y_done()
    sp.xg_send()
    sp.xg_done()
    sp.cg_copy().start()
    sp.cg_copy().wait()
    second_out[...] = g2sum[...]
    basis_out[...] = full_dot(right[...], inverse_factor(g2sum[...]), ((1,), (1,)))


def power(tile, start):
    vm = lambda *shape: pltpu.VMEM(shape, F32)
    its = ITERS + 1
    return pl.pallas_call(
        kernel,
        out_shape=(jax.ShapeDtypeStruct((TC, K), F32), jax.ShapeDtypeStruct((K, K), F32)),
        in_specs=[pl.BlockSpec(memory_space=pltpu.VMEM)] * 2,
        out_specs=[pl.BlockSpec(memory_space=pltpu.VMEM)] * 2,
        scratch_shapes=[
            pltpu.VMEM((TR, TC), BF),
            pltpu.VMEM((TR, TC), BF),
            pltpu.VMEM((TC, TR), BF),
            pltpu.VMEM((TC, TR), BF),
            vm(TC, K),
            pltpu.VMEM((TC, 2 * K), BF),
            vm(TR, K),
            vm(TR, K),
            vm(its, TR // 2, K),
            vm(its, 4, TR // 8, K),
            vm(its, 4, TR // 8, K),
            vm(TR, K),
            vm(TC, K),
            vm(its, 8, ZB, K),
            vm(K, K),
            vm(its, 8, 16, K),
            vm(K, K),
            vm(K, K),
            vm(its, K // 2, K),
            vm(its, 4, K // 8, K),
            vm(its, 4, K // 8, K),
            vm(K, K),
            vm(K, K),
            pltpu.SemaphoreType.DMA((its, SEMS)),
            pltpu.SemaphoreType.DMA((its, SEMS)),
        ],
        compiler_params=pltpu.CompilerParams(
            collective_id=0, has_side_effects=True, vmem_limit_bytes=56 * 2**20
        ),
        name="power",
    )(tile, start)


def body(partials, clip_ratio, start_block):
    summed = lax.psum_scatter(partials[0], "dp", scatter_dimension=1, tiled=True)
    tile = lax.all_to_all(summed, "col", split_axis=1, concat_axis=0, tiled=True)
    vectors, second = power(tile, start_block)
    sigma = jnp.sqrt(jnp.sqrt(jnp.sum(second * second)))
    limit = clip_ratio[0] * (math.sqrt(M) + math.sqrt(N))
    scale = limit / sigma
    update = summed * scale
    return (update, vectors)


def solution(mesh):
    placed = (P("dp", ("row", "col"), None), P(), P(("dp", "col"), None))
    return jax.shard_map(
        body,
        mesh=mesh,
        in_specs=placed,
        out_specs=(P(("row", "col"), "dp"), P(("dp", "col"), None)),
        check_vma=False,
    )
```

```python
import math

import jax
import jax.numpy as jnp
from jax import lax
from jax.experimental import pallas as pl
from jax.experimental.pallas import tpu as pltpu
from jax.sharding import PartitionSpec as P

M = 8192
N = 28672
K = 128
ITERS = 3
TR = 1024
TC = 896
ROWS = 64
HALF = N // 2
CHUNKS = 8
WINDOW = 2
ZB = 112
MESH = pl.DeviceIdType.MESH
BF = jnp.bfloat16
F32 = jnp.float32

G2_CORE, G2_X, G2_Y, G2_XG, G2_CG = 0, 1, 5, 9, 13
L_CORE, L_X, L_Y, L_XG, L_CG = 14, 15, 19, 23, 27
G1_RS, G1_AG, W_RS, W_AG = 28, 36, 44, 52
SEMS = 60


def split2(a):
    hi = a.astype(BF)
    return hi, (a - hi.astype(F32)).astype(BF)


def dot_f32(a, b, dims):
    return lax.dot_general(a, b, (dims, ((), ())), preferred_element_type=F32)


def wide(a):
    hi, lo = split2(a)
    return jnp.concatenate([hi, lo], axis=1)


def full_dot(a, b, dims):
    return lax.dot_general(
        a, b, (dims, ((), ())), precision=lax.Precision.HIGHEST, preferred_element_type=F32
    )


def split_product(hi, lo, both):
    first = jnp.dot(hi, both, preferred_element_type=F32)
    return first[:, :K] + first[:, K:] + jnp.dot(lo, both[:, :K], preferred_element_type=F32)


def inverse_factor(gram):
    lane = lax.broadcasted_iota(jnp.int32, (8, K), 1)
    sub = lax.broadcasted_iota(jnp.int32, (8, K), 0)
    col = lax.broadcasted_iota(jnp.int32, (K, K), 1)
    row = lax.broadcasted_iota(jnp.int32, (K, K), 0)

    def step(k, x):
        p = x[0:8, :]
        q = jnp.where(lane == sub, 1.0, 0.0).astype(F32)
        for j in range(8):
            piv = p[j : j + 1, j : j + 1]
            rs = lax.rsqrt(piv)
            rs = rs * (1.5 - 0.5 * piv * rs * rs)
            urow = p[j : j + 1, :] * rs
            qrow = q[j : j + 1, :] * rs
            m = jnp.where(sub > j, p[:, j : j + 1] * rs, 0.0)
            p = jnp.where(sub == j, urow, p - m * urow)
            q = jnp.where(sub == j, qrow, q - m * qrow)
        y = jnp.where(lane < 8, q, p)
        left = jnp.where((lane >= 8) & (lane < K - 8 * k), p, 0.0)

        def split3(a):
            hi = a.astype(BF).astype(F32)
            mid = (a - hi).astype(BF).astype(F32)
            return hi, mid, a - hi - mid

        lh, lm, ll = split3(left)
        yh, ym, yl = split3(y)
        a = jnp.concatenate([lh, lh, lm, lh, ll, lm], axis=0).astype(BF)
        b = jnp.concatenate([yh, ym, yh, yl, yh, ym], axis=0).astype(BF)
        upd = dot_f32(a, b, ((0,), (0,)))
        new = jnp.where(col < 8, 0.0, x) - upd
        new = jnp.where(row < K - 8 * k, new, x)
        return pltpu.roll(jnp.concatenate([new[8:, :], y], axis=0), K - 8, axis=1)

    x = lax.fori_loop(0, K // 8, step, gram)
    return jnp.where(col <= row, x, 0.0)


def kernel(
    partial,
    start,
    basis_out,
    second_out,
    summed_out,
    own,
    theirs,
    summed,
    tile,
    dp_send,
    dp_recv,
    own_sem,
    out_sem,
    tile_send,
    tile_recv,
    start_sem,
    end_sem,
    moved,
    thi,
    tlo,
    thit,
    tlot,
    right,
    rwide,
    left,
    lpart,
    lcore,
    lx,
    ly,
    lsum,
    wpart,
    wz,
    gram1,
    g1z,
    g1share,
    gram2,
    g2core,
    g2x,
    g2y,
    g2sum,
    factor,
    send,
    recv,
):
    d = lax.axis_index("dp")
    z = lax.axis_index("row")
    c = lax.axis_index("col")
    co = lax.rem(c, 2)
    yl = lax.rem(lax.div(c, 2), 2)
    x = lax.div(c, 4)
    zl = lax.rem(z, 2)
    zh = lax.div(z, 2)
    y = d * 2 + zl
    p = yl * 4 + zh
    j = x * 4 + zl * 2 + co

    def dev_core():
        return (d, z, c + 1 - 2 * co)

    def dev_x(i):
        return (d, z, i * 4 + yl * 2 + co)

    def dev_y(i):
        return (lax.div(i, 2), zh * 2 + lax.rem(i, 2), c)

    def dev_p(i):
        return (d, lax.rem(i, 4) * 2 + zl, x * 4 + lax.div(i, 4) * 2 + co)

    def dev_j(i):
        return (d, zh * 2 + lax.rem(lax.div(i, 2), 2), lax.div(i, 4) * 4 + yl * 2 + lax.rem(i, 2))

    partner = (1 - d, z, c)
    across = (d, z, x * 4 + (1 - yl) * 2 + co)
    above = (d, lax.rem(z + 1, 8), c)
    below = (d, lax.rem(z + 7, 8), c)

    barrier = pltpu.get_barrier_semaphore()
    peers = [partner, across, above, below]
    peers += [dev_y(lax.rem(y + o, 4)) for o in (1, 3, 2)]
    peers += [dev_p(lax.rem(p + o, 8)) for o in (1, 7, 2, 6, 3, 5, 4)]
    peers += [dev_j(lax.rem(j + o, 16)) for o in range(1, 16)]
    for dev in peers:
        pl.semaphore_signal(barrier, inc=1, device_id=dev, device_id_type=MESH)

    def own_copy(k):
        rows = pl.ds(pl.multiple_of(k * 8, 8), 8)
        mine = pl.ds(pl.multiple_of(d * HALF, HALF), HALF)
        return pltpu.make_async_copy(partial.at[rows, mine], own.at[rows, :], own_sem.at[k])

    def dp_copy(k):
        rows = pl.ds(pl.multiple_of(k * 8, 8), 8)
        other = pl.ds(pl.multiple_of((1 - d) * HALF, HALF), HALF)
        return pltpu.make_async_remote_copy(
            src_ref=partial.at[rows, other],
            dst_ref=theirs.at[rows, :],
            send_sem=dp_send.at[k],
            recv_sem=dp_recv.at[k],
            device_id=partner,
            device_id_type=MESH,
        )

    start_here = pltpu.make_async_copy(start, right, start_sem.at[0])
    start_across = pltpu.make_async_remote_copy(
        src_ref=start,
        dst_ref=right,
        send_sem=start_sem.at[1],
        recv_sem=start_sem.at[2],
        device_id=across,
        device_id_type=MESH,
    )

    for k in range(CHUNKS):
        own_copy(k).start()
    pl.semaphore_wait(barrier, len(peers))
    for k in range(WINDOW):
        dp_copy(k).start()

    @pl.when(yl == zl)
    def _():
        start_here.start()

    def prepare(k):
        rows = pl.ds(pl.multiple_of(k * 128, 128), 128)
        got = tile.at[pl.ds(0, 120), :]
        pltpu.make_async_copy(got, got, tile_recv.at[k]).wait()
        part = tile[rows, :]
        hi, lo = split2(part)
        thi[rows, :] = hi
        tlo[rows, :] = lo
        hi, lo = split2(part.T)
        thit[:, rows] = hi
        tlot[:, rows] = lo

    def chunk(k, carry):
        rows = pl.ds(pl.multiple_of(k * 8, 8), 8)
        place = pl.ds(pl.multiple_of(k * 128 + j * 8, 8), 8)
        dp_copy(k).wait()

        @pl.when(k + WINDOW < CHUNKS)
        def _():
            dp_copy(k + WINDOW).start()

        @pl.when((k == CHUNKS - 1) & (yl == zl))
        def _():
            start_across.start()

        own_copy(k).wait()
        summed[rows, :] = own[rows, :] + theirs[rows, :]

        def block(i):
            return summed.at[rows, pl.ds(pl.multiple_of(i * TC, 128), TC)]

        for o in range(1, 16):
            i = lax.rem(j + o, 16)
            pltpu.make_async_remote_copy(
                src_ref=block(i),
                dst_ref=tile.at[place, :],
                send_sem=tile_send.at[k],
                recv_sem=tile_recv.at[k],
                device_id=dev_j(i),
                device_id_type=MESH,
            ).start()
        tile[place, :] = block(j)[...]

        @pl.when(k > 0)
        def _():
            prepare(k - 1)

        return carry

    lax.fori_loop(0, CHUNKS, chunk, 0)
    out_copy = pltpu.make_async_copy(summed, summed_out, out_sem)
    out_copy.start()
    prepare(CHUNKS - 1)
    for k in range(CHUNKS):
        sent = tile.at[pl.ds(0, 120), :]
        pltpu.make_async_copy(sent, sent, tile_send.at[k]).wait()

    @pl.when(yl == zl)
    def _():
        start_here.wait()
        start_across.wait_send()

    @pl.when(yl != zl)
    def _():
        start_across.wait_recv()

    right[...] = right[...] * math.sqrt(3.0 / N)
    rwide[...] = wide(right[...])

    def copy(src, dst, it, slot_out, slot_in, dev):
        return pltpu.make_async_remote_copy(
            src_ref=src,
            dst_ref=dst,
            send_sem=send.at[it, slot_out],
            recv_sem=recv.at[it, slot_in],
            device_id=dev,
            device_id_type=MESH,
        )

    def ring(n, me, dev, base, it, src, dst):
        for o in sorted(range(1, n), key=lambda o: min(o, n - o)):
            i = lax.rem(me + o, n)
            copy(src(i), dst(me), it, base + o, base + o, dev(i)).start()

    def ring_wait(n, me, dev, base, it, src, dst):
        for o in sorted(range(1, n), key=lambda o: min(o, n - o)):
            i = lax.rem(me + n - o, n)
            copy(src(i), dst(i), it, base + o, base + o, dev(i)).wait()

    def blocks(ref, size):
        return lambda i: ref.at[pl.ds(pl.multiple_of(i * size, size), size), :]

    class Plane:
        def __init__(self, it, rows, part, core_buf, x_buf, y_buf, total, sems):
            self.it, self.rows = it, rows
            self.part, self.core_buf, self.x_buf, self.y_buf, self.total = part, core_buf, x_buf, y_buf, total
            self.s_core, self.s_x, self.s_y, self.s_xg, self.s_cg = sems
            self.half, self.unit = rows // 2, rows // 8

        def mine(self):
            return pl.ds(pl.multiple_of(co * self.half + x * self.unit, self.unit), self.unit)

        def core_copy(self):
            there = pl.ds(pl.multiple_of((1 - co) * self.half, self.half), self.half)
            return copy(self.part.at[there, :], self.core_buf.at[self.it], self.it, self.s_core, self.s_core, dev_core())

        def core_done(self):
            self.core_copy().wait()
            here = pl.ds(pl.multiple_of(co * self.half, self.half), self.half)
            self.core_buf[self.it] = self.core_buf[self.it] + self.part[here, :]

        def x_args(self):
            src = lambda i: self.core_buf.at[self.it, pl.ds(pl.multiple_of(i * self.unit, self.unit), self.unit), :]
            return (4, x, dev_x, self.s_x, self.it, src, lambda i: self.x_buf.at[self.it, i])

        def x_send(self):
            own = self.core_buf[self.it, pl.ds(pl.multiple_of(x * self.unit, self.unit), self.unit), :]
            self.x_buf[self.it, x] = own
            ring(*self.x_args())

        def x_done(self):
            ring_wait(*self.x_args())
            self.y_buf[self.it, y] = (self.x_buf[self.it, 0] + self.x_buf[self.it, 1]) + (
                self.x_buf[self.it, 2] + self.x_buf[self.it, 3]
            )

        def y_args(self):
            return (
                4,
                y,
                dev_y,
                self.s_y,
                self.it,
                lambda i: self.y_buf.at[self.it, y],
                lambda i: self.y_buf.at[self.it, i],
            )

        def y_send(self):
            ring(*self.y_args())

        def y_done(self):
            ring_wait(*self.y_args())
            self.total[self.mine(), :] = (self.y_buf[self.it, 0] + self.y_buf[self.it, 1]) + (
                self.y_buf[self.it, 2] + self.y_buf[self.it, 3]
            )

        def xg_args(self):
            place = lambda i: self.total.at[pl.ds(pl.multiple_of(co * self.half + i * self.unit, self.unit), self.unit), :]
            return (4, x, dev_x, self.s_xg, self.it, lambda i: place(x), place)

        def xg_send(self):
            ring(*self.xg_args())

        def xg_done(self):
            ring_wait(*self.xg_args())

        def cg_copy(self):
            here = self.total.at[pl.ds(pl.multiple_of(co * self.half, self.half), self.half), :]
            return copy(here, here, self.it, self.s_cg, self.s_cg, dev_core())

    def left_plane(it):
        return Plane(it, TR, lpart, lcore, lx, ly, lsum, (L_CORE, L_X, L_Y, L_XG, L_CG))

    def second_plane(it):
        return Plane(it, K, gram2, g2core, g2x, g2y, g2sum, (G2_CORE, G2_X, G2_Y, G2_XG, G2_CG))

    def iteration(it, carry):
        lp, sp = left_plane(it), second_plane(it)

        @pl.when(it > 0)
        def _():
            gram2[...] = full_dot(right[...], right[...], ((0,), (0,)))
            sp.core_copy().start()

        lpart[...] = split_product(thi[...], tlo[...], rwide[...])
        lp.core_copy().start()

        @pl.when(it > 0)
        def _():
            sp.core_done()
            sp.x_send()

        lp.core_done()
        lp.x_send()

        @pl.when(it > 0)
        def _():
            sp.x_done()
            sp.y_send()

        lp.x_done()
        lp.y_send()

        @pl.when(it > 0)
        def _():
            sp.y_done()
            sp.xg_send()

        lp.y_done()
        lp.xg_send()

        @pl.when(it > 0)
        def _():
            sp.xg_done()
            sp.cg_copy().start()

        lp.xg_done()
        lp.cg_copy().start()

        @pl.when(it > 0)
        def _():
            sp.cg_copy().wait()
            factor[...] = inverse_factor(g2sum[...])

        lp.cg_copy().wait()

        @pl.when(it == 0)
        def _():
            left[...] = lsum[...]

        @pl.when(it > 0)
        def _():
            left[...] = full_dot(lsum[...], factor[...], ((1,), (1,)))

        gram1[...] = full_dot(left[...], left[...], ((0,), (0,)))
        g1_rs = (8, p, dev_p, G1_RS, it, blocks(gram1, 16), lambda i: g1z.at[it, i])
        g1z[it, p] = gram1[pl.ds(pl.multiple_of(p * 16, 16), 16), :]
        ring(*g1_rs)

        lwide = wide(left[...])
        wpart[...] = split_product(thit[...], tlot[...], lwide)
        w_rs = (8, p, dev_p, W_RS, it, blocks(wpart, ZB), lambda i: wz.at[it, i])
        wz[it, p] = wpart[pl.ds(pl.multiple_of(p * ZB, 16), ZB), :]
        ring(*w_rs)

        ring_wait(*g1_rs)
        total = g1z[it, 0]
        for i in range(1, 8):
            total = total + g1z[it, i]
        g1share[pl.ds(pl.multiple_of(p * 16, 16), 16), :] = total
        share = blocks(g1share, 16)
        g1_ag = (8, p, dev_p, G1_AG, it, lambda i: share(p), share)
        ring(*g1_ag)

        ring_wait(*w_rs)
        total = wz[it, 0]
        for i in range(1, 8):
            total = total + wz[it, i]
        right[pl.ds(pl.multiple_of(p * ZB, 16), ZB), :] = total
        place = blocks(right, ZB)
        w_ag = (8, p, dev_p, W_AG, it, lambda i: place(p), place)
        ring(*w_ag)

        ring_wait(*g1_ag)
        factor[...] = inverse_factor(g1share[...])
        ring_wait(*w_ag)
        right[...] = full_dot(right[...], factor[...], ((1,), (1,)))
        rwide[...] = wide(right[...])
        return carry

    lax.fori_loop(0, ITERS, iteration, 0)

    sp = second_plane(ITERS)
    gram2[...] = full_dot(right[...], right[...], ((0,), (0,)))
    sp.core_copy().start()
    sp.core_done()
    sp.x_send()
    sp.x_done()
    sp.y_send()
    sp.y_done()
    sp.xg_send()
    sp.xg_done()
    sp.cg_copy().start()
    sp.cg_copy().wait()
    second_out[...] = g2sum[...]
    right[...] = full_dot(right[...], inverse_factor(g2sum[...]), ((1,), (1,)))

    def end_copy(i, dev):
        rows = pl.ds(i * (TC // 2), TC // 2)
        return pltpu.make_async_remote_copy(
            src_ref=right.at[rows, :],
            dst_ref=moved.at[rows, :],
            send_sem=end_sem.at[i],
            recv_sem=end_sem.at[2 + i],
            device_id=dev,
            device_id_type=MESH,
        )

    ends = [end_copy(0, above), end_copy(1, below)]

    @pl.when(yl == zl)
    def _():
        for e in ends:
            e.start()
        basis_out[...] = right[...]
        for e in ends:
            e.wait_send()

    @pl.when(yl != zl)
    def _():
        for e in ends:
            e.wait_recv()
        basis_out[...] = moved[...]

    out_copy.wait()


def power(partial, start):
    vm = lambda *shape: pltpu.VMEM(shape, F32)
    its = ITERS + 1
    return pl.pallas_call(
        kernel,
        out_shape=(
            jax.ShapeDtypeStruct((TC, K), F32),
            jax.ShapeDtypeStruct((K, K), F32),
            jax.ShapeDtypeStruct((ROWS, HALF), F32),
        ),
        in_specs=[pl.BlockSpec(memory_space=pl.ANY)] * 2,
        out_specs=[pl.BlockSpec(memory_space=pltpu.VMEM)] * 2 + [pl.BlockSpec(memory_space=pl.ANY)],
        scratch_shapes=[
            vm(ROWS, HALF),
            vm(ROWS, HALF),
            vm(ROWS, HALF),
            vm(TR, TC),
            pltpu.SemaphoreType.DMA((CHUNKS,)),
            pltpu.SemaphoreType.DMA((CHUNKS,)),
            pltpu.SemaphoreType.DMA((CHUNKS,)),
            pltpu.SemaphoreType.DMA,
            pltpu.SemaphoreType.DMA((CHUNKS,)),
            pltpu.SemaphoreType.DMA((CHUNKS,)),
            pltpu.SemaphoreType.DMA((3,)),
            pltpu.SemaphoreType.DMA((4,)),
            vm(TC, K),
            pltpu.VMEM((TR, TC), BF),
            pltpu.VMEM((TR, TC), BF),
            pltpu.VMEM((TC, TR), BF),
            pltpu.VMEM((TC, TR), BF),
            vm(TC, K),
            pltpu.VMEM((TC, 2 * K), BF),
            vm(TR, K),
            vm(TR, K),
            vm(its, TR // 2, K),
            vm(its, 4, TR // 8, K),
            vm(its, 4, TR // 8, K),
            vm(TR, K),
            vm(TC, K),
            vm(its, 8, ZB, K),
            vm(K, K),
            vm(its, 8, 16, K),
            vm(K, K),
            vm(K, K),
            vm(its, K // 2, K),
            vm(its, 4, K // 8, K),
            vm(its, 4, K // 8, K),
            vm(K, K),
            vm(K, K),
            pltpu.SemaphoreType.DMA((its, SEMS)),
            pltpu.SemaphoreType.DMA((its, SEMS)),
        ],
        compiler_params=pltpu.CompilerParams(
            collective_id=0, has_side_effects=True, vmem_limit_bytes=60 * 2**20
        ),
        name="power",
    )(partial, start)


def body(partials, clip_ratio, start_block):
    vectors, second, summed = power(partials[0], start_block)
    sigma = jnp.sqrt(jnp.sqrt(jnp.sum(second * second)))
    limit = clip_ratio[0] * (math.sqrt(M) + math.sqrt(N))
    scale = limit / sigma
    update = summed * scale
    return (update, vectors)


def solution(mesh):
    placed = (P("dp", ("row", "col"), None), P(), P(("dp", "col"), None))
    return jax.shard_map(
        body,
        mesh=mesh,
        in_specs=placed,
        out_specs=(P(("row", "col"), "dp"), P(("dp", "col"), None)),
        check_vma=False,
    )
```

```python
import math

import jax
import jax.numpy as jnp
from jax import lax
from jax.experimental import pallas as pl
from jax.experimental.pallas import tpu as pltpu
from jax.sharding import PartitionSpec as P

M = 8192
N = 28672
K = 128
ITERS = 3
TR = 1024
TC = 896
ROWS = 64
HALF = N // 2
CHUNKS = 8
PANEL = 16
WINDOW = 2
ZB = 112
MESH = pl.DeviceIdType.MESH
BF = jnp.bfloat16
F32 = jnp.float32

G2_CORE, G2_X, G2_Y, G2_CG = 0, 1, 5, 9
L_CORE, L_X, L_Y, L_XG, L_CG = 10, 11, 15, 19, 23
G1_RS, G1_AG, G1_CG, W_RS, W_AG = 24, 32, 40, 41, 49
SEMS = 57


def split2(a):
    hi = a.astype(BF)
    return hi, (a - hi.astype(F32)).astype(BF)


def dot_f32(a, b, dims):
    return lax.dot_general(a, b, (dims, ((), ())), preferred_element_type=F32)


def wide(a):
    hi, lo = split2(a)
    return jnp.concatenate([hi, lo], axis=1)


def full_dot(a, b, dims):
    return lax.dot_general(
        a, b, (dims, ((), ())), precision=lax.Precision.HIGHEST, preferred_element_type=F32
    )


def split_product(hi, lo, both):
    first = jnp.dot(hi, both, preferred_element_type=F32)
    return first[:, :K] + first[:, K:] + jnp.dot(lo, both[:, :K], preferred_element_type=F32)


def inverse_factor(gram):
    lane = lax.broadcasted_iota(jnp.int32, (PANEL, K), 1)
    sub = lax.broadcasted_iota(jnp.int32, (PANEL, K), 0)
    col = lax.broadcasted_iota(jnp.int32, (K, K), 1)
    row = lax.broadcasted_iota(jnp.int32, (K, K), 0)

    def split3(a):
        hi = a.astype(BF).astype(F32)
        mid = (a - hi).astype(BF).astype(F32)
        return hi, mid, a - hi - mid

    def step(k, x):
        p = x[0:PANEL, :]
        cols = [jnp.broadcast_to(p[:, i : i + 1], (PANEL, K)) for i in range(PANEL)]
        pivots = []
        for j in range(PANEL):
            heads = [cols[i][j : j + 1, :] for i in range(j, PANEL)]
            pivots.append(heads[0])
            m = jnp.where(sub > j, cols[j] * (1.0 / heads[0]), 0.0)
            for i in range(j + 1, PANEL):
                cols[i] = cols[i] - m * heads[i - j]
            head = jnp.where(lane[:1] == j, 1.0, p[j : j + 1, :])
            p = jnp.where((lane == j) & (sub > j), 0.0, p) - m * head
        pivot = jnp.concatenate(pivots, axis=0)
        rs = lax.rsqrt(pivot)
        rs = rs * (1.5 - 0.5 * pivot * rs * rs)
        p = jnp.where(lane == sub, 1.0, p) * rs
        y = jnp.where((lane < PANEL) & (lane > sub), 0.0, p)
        lead = jnp.where((lane >= PANEL) & (lane < K - PANEL * k), p, 0.0)
        lh, lm, ll = split3(lead)
        yh, ym, yl = split3(y)
        a = jnp.concatenate([lh, lh, lm, lh, ll, lm], axis=0).astype(BF)
        b = jnp.concatenate([yh, ym, yh, yl, yh, ym], axis=0).astype(BF)
        new = jnp.where(col < PANEL, 0.0, x) - dot_f32(a, b, ((0,), (0,)))
        new = jnp.where(row < K - PANEL * k, new, x)
        return pltpu.roll(jnp.concatenate([new[PANEL:, :], y], axis=0), K - PANEL, axis=1)

    x = lax.fori_loop(0, K // PANEL, step, gram)
    return jnp.where(col <= row, x, 0.0)


def kernel(
    partial,
    clip_ratio,
    start,
    basis_out,
    scale_out,
    summed_out,
    own,
    theirs,
    summed,
    tile,
    dp_send,
    dp_recv,
    own_sem,
    out_sem,
    tile_send,
    tile_recv,
    start_sem,
    moved,
    mine,
    thi,
    tlo,
    thit,
    tlot,
    right,
    rwide,
    left,
    lpart,
    lcore,
    lx,
    ly,
    lsum,
    wpart,
    wz,
    gram1,
    g1z,
    g1share,
    gram2,
    g2core,
    g2x,
    g2y,
    g2sum,
    factor,
    send,
    recv,
):
    d = lax.axis_index("dp")
    z = lax.axis_index("row")
    c = lax.axis_index("col")
    co = lax.rem(c, 2)
    yl = lax.rem(lax.div(c, 2), 2)
    x = lax.div(c, 4)
    zl = lax.rem(z, 2)
    zh = lax.div(z, 2)
    y = d * 2 + zl
    p = yl * 4 + zh
    j = x * 4 + zl * 2 + co

    def dev_core():
        return (d, z, c + 1 - 2 * co)

    def dev_x(i):
        return (d, z, i * 4 + yl * 2 + co)

    def dev_y(i):
        return (lax.div(i, 2), zh * 2 + lax.rem(i, 2), c)

    def dev_p(i):
        return (d, lax.rem(i, 4) * 2 + zl, x * 4 + lax.div(i, 4) * 2 + co)

    def dev_j(i):
        return (d, zh * 2 + lax.rem(lax.div(i, 2), 2), lax.div(i, 4) * 4 + yl * 2 + lax.rem(i, 2))

    partner = (1 - d, z, c)
    across = (d, z, x * 4 + (1 - yl) * 2 + co)

    def dev_end_y(i):
        return (lax.div(i, 2), z, x * 4 + lax.rem(i, 2) * 2 + co)

    def dev_yz(i):
        return (d, lax.rem(i, 8), x * 4 + lax.div(i, 8) * 2 + co)

    barrier = pltpu.get_barrier_semaphore()
    peers = [dev_y(lax.rem(y + o, 4)) for o in (1, 3, 2)]
    peers += [dev_end_y(lax.rem(d * 2 + yl + o, 4)) for o in (1, 3, 2)]
    peers += [dev_yz(lax.rem(yl * 8 + z + o, 16)) for o in range(1, 16)]
    peers += [dev_j(lax.rem(j + o, 16)) for o in range(1, 16)]
    for dev in peers:
        pl.semaphore_signal(barrier, inc=1, device_id=dev, device_id_type=MESH)

    def part_of(k, h, base):
        rows = pl.ds(pl.multiple_of(k * 8, 8), 8)
        return rows, pl.ds(pl.multiple_of(base + h * (HALF // 2), 128), HALF // 2)

    def own_copy(k):
        rows = pl.ds(pl.multiple_of(k * 8, 8), 8)
        mine = pl.ds(pl.multiple_of(d * HALF, HALF), HALF)
        return pltpu.make_async_copy(partial.at[rows, mine], own.at[rows, :], own_sem.at[k])

    def dp_copy(k, turn):
        h = lax.rem(turn + lax.div(x, 2), 2)
        rows, other = part_of(k, h, (1 - d) * HALF)
        return pltpu.make_async_remote_copy(
            src_ref=partial.at[rows, other],
            dst_ref=theirs.at[rows, part_of(k, h, 0)[1]],
            send_sem=dp_send.at[2 * k + turn],
            recv_sem=dp_recv.at[2 * k + turn],
            device_id=partner,
            device_id_type=MESH,
        )

    start_here = pltpu.make_async_copy(start, right, start_sem.at[0])
    start_across = pltpu.make_async_remote_copy(
        src_ref=start,
        dst_ref=right,
        send_sem=start_sem.at[1],
        recv_sem=start_sem.at[2],
        device_id=across,
        device_id_type=MESH,
    )

    for k in range(CHUNKS):
        own_copy(k).start()
    pl.semaphore_wait(barrier, len(peers))
    for k in range(WINDOW):
        dp_copy(k, 0).start()
        dp_copy(k, 1).start()

    @pl.when(yl == zl)
    def _():
        start_here.start()

    def prepare(k):
        rows = pl.ds(pl.multiple_of(k * 128, 128), 128)
        got = tile.at[pl.ds(0, 120), :]
        pltpu.make_async_copy(got, got, tile_recv.at[k]).wait()
        part = tile[rows, :]
        hi, lo = split2(part)
        thi[rows, :] = hi
        tlo[rows, :] = lo
        hi, lo = split2(part.T)
        thit[:, rows] = hi
        tlot[:, rows] = lo

    def chunk(k, carry):
        rows = pl.ds(pl.multiple_of(k * 8, 8), 8)
        place = pl.ds(pl.multiple_of(k * 128 + j * 8, 8), 8)
        own_copy(k).wait()
        for turn in (0, 1):
            dp_copy(k, turn).wait()

            @pl.when(k + WINDOW < CHUNKS)
            def _():
                dp_copy(k + WINDOW, turn).start()

            h = lax.rem(turn + lax.div(x, 2), 2)
            half = part_of(k, h, 0)[1]
            summed[rows, half] = own[rows, half] + theirs[rows, half]

            def block(i):
                return summed.at[rows, pl.ds(pl.multiple_of(i * TC, 128), TC)]

            def send_block(o):
                i = h * 8 + lax.rem(j + o, 8)
                pltpu.make_async_remote_copy(
                    src_ref=block(i),
                    dst_ref=tile.at[place, :],
                    send_sem=tile_send.at[k],
                    recv_sem=tile_recv.at[k],
                    device_id=dev_j(i),
                    device_id_type=MESH,
                ).start()

            if turn == 0:
                tile[place, :] = block(j)[...]
            else:
                send_block(0)
            for o in range(1, 8):
                send_block(o)

        @pl.when((k == CHUNKS - WINDOW) & (yl == zl))
        def _():
            start_across.start()

        @pl.when(k > 0)
        def _():
            prepare(k - 1)

        return carry

    lax.fori_loop(0, CHUNKS, chunk, 0)
    out_copy = pltpu.make_async_copy(summed, summed_out, out_sem)
    out_copy.start()
    prepare(CHUNKS - 1)
    for k in range(CHUNKS):
        sent = tile.at[pl.ds(0, 120), :]
        pltpu.make_async_copy(sent, sent, tile_send.at[k]).wait()

    @pl.when(yl == zl)
    def _():
        start_here.wait()
        start_across.wait_send()

    @pl.when(yl != zl)
    def _():
        start_across.wait_recv()

    right[...] = right[...] * math.sqrt(3.0 / N)
    rwide[...] = wide(right[...])

    def copy(src, dst, it, slot_out, slot_in, dev):
        return pltpu.make_async_remote_copy(
            src_ref=src,
            dst_ref=dst,
            send_sem=send.at[it, slot_out],
            recv_sem=recv.at[it, slot_in],
            device_id=dev,
            device_id_type=MESH,
        )

    def ring(n, me, dev, base, it, src, dst):
        for o in sorted(range(1, n), key=lambda o: min(o, n - o)):
            i = lax.rem(me + o, n)
            copy(src(i), dst(me), it, base + o, base + o, dev(i)).start()

    def ring_wait(n, me, dev, base, it, src, dst):
        for o in sorted(range(1, n), key=lambda o: min(o, n - o)):
            i = lax.rem(me + n - o, n)
            copy(src(i), dst(i), it, base + o, base + o, dev(i)).wait()

    def blocks_at(i, size):
        return pl.ds(pl.multiple_of(i * size, 8), size)

    def blocks(ref, size):
        return lambda i: ref.at[pl.ds(pl.multiple_of(i * size, size), size), :]

    class Plane:
        def __init__(self, it, rows, part, core_buf, x_buf, y_buf, total, sems, y, dev_y):
            self.it, self.rows, self.y, self.dev_y = it, rows, y, dev_y
            self.part, self.core_buf, self.x_buf, self.y_buf, self.total = part, core_buf, x_buf, y_buf, total
            self.s_core, self.s_x, self.s_y, self.s_xg, self.s_cg = sems
            self.half, self.unit = rows // 2, rows // 8

        def mine(self):
            return pl.ds(pl.multiple_of(co * self.half + x * self.unit, self.unit), self.unit)

        def core_copy(self):
            there = pl.ds(pl.multiple_of((1 - co) * self.half, self.half), self.half)
            return copy(self.part.at[there, :], self.core_buf.at[self.it], self.it, self.s_core, self.s_core, dev_core())

        def core_done(self):
            self.core_copy().wait()
            here = pl.ds(pl.multiple_of(co * self.half, self.half), self.half)
            self.core_buf[self.it] = self.core_buf[self.it] + self.part[here, :]

        def x_args(self):
            src = lambda i: self.core_buf.at[self.it, pl.ds(pl.multiple_of(i * self.unit, self.unit), self.unit), :]
            return (4, x, dev_x, self.s_x, self.it, src, lambda i: self.x_buf.at[self.it, i])

        def x_send(self):
            own = self.core_buf[self.it, pl.ds(pl.multiple_of(x * self.unit, self.unit), self.unit), :]
            self.x_buf[self.it, x] = own
            ring(*self.x_args())

        def x_done(self):
            ring_wait(*self.x_args())
            self.y_buf[self.it, self.y] = (self.x_buf[self.it, 0] + self.x_buf[self.it, 1]) + (
                self.x_buf[self.it, 2] + self.x_buf[self.it, 3]
            )

        def y_args(self):
            return (
                4,
                self.y,
                self.dev_y,
                self.s_y,
                self.it,
                lambda i: self.y_buf.at[self.it, self.y],
                lambda i: self.y_buf.at[self.it, i],
            )

        def y_send(self):
            ring(*self.y_args())

        def y_done(self):
            ring_wait(*self.y_args())
            self.total[self.mine(), :] = (self.y_buf[self.it, 0] + self.y_buf[self.it, 1]) + (
                self.y_buf[self.it, 2] + self.y_buf[self.it, 3]
            )

        def xg_args(self):
            place = lambda i: self.total.at[pl.ds(pl.multiple_of(co * self.half + i * self.unit, self.unit), self.unit), :]
            return (4, x, dev_x, self.s_xg, self.it, lambda i: place(x), place)

        def xg_send(self):
            ring(*self.xg_args())

        def xg_done(self):
            ring_wait(*self.xg_args())

        def cg_copy(self):
            here = self.total.at[pl.ds(pl.multiple_of(co * self.half, self.half), self.half), :]
            return copy(here, here, self.it, self.s_cg, self.s_cg, dev_core())

    class Small(Plane):
        def mine(self):
            return pl.ds(pl.multiple_of(co * self.half, self.half), self.half)

        def x_args(self):
            return (4, x, dev_x, self.s_x, self.it, lambda i: self.x_buf.at[self.it, x], lambda i: self.x_buf.at[self.it, i])

        def x_send(self):
            self.x_buf[self.it, x] = self.core_buf[self.it]
            ring(*self.x_args())

    def left_plane(it):
        return Plane(it, TR, lpart, lcore, lx, ly, lsum, (L_CORE, L_X, L_Y, L_XG, L_CG), y, dev_y)

    def second_plane(it, y=y, dev_y=dev_y):
        return Small(it, K, gram2, g2core, g2x, g2y, g2sum, (G2_CORE, G2_X, G2_Y, None, G2_CG), y, dev_y)

    def iteration(it, carry):
        lp, sp = left_plane(it), second_plane(it)

        @pl.when(it > 0)
        def _():
            gram2[...] = full_dot(right[...], right[...], ((0,), (0,)))
            sp.core_copy().start()

        for half in (1 - co, co):
            rows = pl.ds(pl.multiple_of(half * (TR // 2), TR // 2), TR // 2)
            lpart[rows, :] = split_product(thi[rows, :], tlo[rows, :], rwide[...])
            if half is not co:
                lp.core_copy().start()

        @pl.when(it > 0)
        def _():
            sp.core_done()
            sp.x_send()

        lp.core_done()
        lp.x_send()

        @pl.when(it > 0)
        def _():
            sp.x_done()
            sp.y_send()

        lp.x_done()
        lp.y_send()

        @pl.when(it > 0)
        def _():
            sp.y_done()
            sp.cg_copy().start()

        lp.y_done()
        lp.xg_send()

        lp.xg_done()
        lp.cg_copy().start()

        @pl.when(it > 0)
        def _():
            sp.cg_copy().wait()
            factor[...] = inverse_factor(g2sum[...])

        lp.cg_copy().wait()

        @pl.when(it == 0)
        def _():
            left[...] = lsum[...]

        @pl.when(it > 0)
        def _():
            left[...] = full_dot(lsum[...], factor[...], ((1,), (1,)))

        gram1[...] = full_dot(left[...], left[...], ((0,), (0,)))
        half = pl.ds(pl.multiple_of(co * (K // 2), K // 2), K // 2)
        part = gram1.at[half, :]
        g1_rs = (8, p, dev_p, G1_RS, it, blocks(part, 8), lambda i: g1z.at[it, i])
        g1z[it, p] = gram1[pl.ds(pl.multiple_of(co * (K // 2) + p * 8, 8), 8), :]
        ring(*g1_rs)

        lwide = wide(left[...])
        w_rs = (8, p, dev_p, W_RS, it, blocks(wpart, ZB), lambda i: wz.at[it, i])
        for turn in (0, 1):
            h = lax.rem(yl + turn, 2)
            rows = pl.ds(pl.multiple_of(h * (TC // 2), TC // 2), TC // 2)
            wpart[rows, :] = split_product(thit[rows, :], tlot[rows, :], lwide)
            if turn == 0:
                wz[it, p] = wpart[pl.ds(pl.multiple_of(p * ZB, 16), ZB), :]
            for o in (0, 1, 3, 2)[1 - turn :]:
                i = h * 4 + lax.rem(zh + o, 4)
                far = lax.rem(i + 8 - p, 8)
                copy(wpart.at[blocks_at(i, ZB), :], wz.at[it, p], it, W_RS + far, W_RS + far, dev_p(i)).start()

        ring_wait(*g1_rs)
        total = g1z[it, 0]
        for i in range(1, 8):
            total = total + g1z[it, i]
        g1share[pl.ds(pl.multiple_of(co * (K // 2) + p * 8, 8), 8), :] = total
        share = blocks(g1share.at[half, :], 8)
        g1_ag = (8, p, dev_p, G1_AG, it, lambda i: share(p), share)
        ring(*g1_ag)

        ring_wait(*w_rs)
        total = wz[it, 0]
        for i in range(1, 8):
            total = total + wz[it, i]

        place = blocks(right, ZB)
        w_ag = (8, p, dev_p, W_AG, it, lambda i: place(p), place)
        end_place = blocks(moved, ZB)

        def end_send(i):
            return copy(mine, end_place(p), it, W_AG + i, W_AG + p, (d, i, x * 4 + zl * 2 + co))

        def end_recv(i):
            sender = (d, lax.rem(i, 4) * 2 + yl, x * 4 + lax.div(i, 4) * 2 + co)
            return copy(mine, end_place(i), it, W_AG + i, W_AG + i, sender)

        @pl.when(it < ITERS - 1)
        def _():
            right[blocks_at(p, ZB), :] = total
            ring(*w_ag)

        @pl.when(it == ITERS - 1)
        def _():
            mine[...] = total
            for i in range(8):

                @pl.when((i != z) | (yl != zl))
                def _(i=i):
                    end_send(i).start()

            @pl.when(yl == zl)
            def _():
                moved[blocks_at(p, ZB), :] = total

        ring_wait(*g1_ag)
        swap = copy(g1share.at[half, :], g1share.at[half, :], it, G1_CG, G1_CG, dev_core())
        swap.start()
        swap.wait()
        factor[...] = inverse_factor(g1share[...])

        @pl.when(it < ITERS - 1)
        def _():
            ring_wait(*w_ag)
            right[...] = full_dot(right[...], factor[...], ((1,), (1,)))

        @pl.when(it == ITERS - 1)
        def _():
            for i in range(8):

                @pl.when((i != z) | (yl != zl))
                def _(i=i):
                    end_send(i).wait_send()

                @pl.when((i != p) | (yl != zl))
                def _(i=i):
                    end_recv(i).wait_recv()

            right[...] = full_dot(moved[...], factor[...], ((1,), (1,)))

        rwide[...] = wide(right[...])
        return carry

    lax.fori_loop(0, ITERS, iteration, 0)

    sp = second_plane(ITERS, d * 2 + yl, dev_end_y)
    gram2[...] = full_dot(right[...], right[...], ((0,), (0,)))
    sp.core_copy().start()
    sp.core_done()
    sp.x_send()
    sp.x_done()
    sp.y_send()
    sp.y_done()
    sp.cg_copy().start()
    sp.cg_copy().wait()
    second = g2sum[...]
    sigma = jnp.sqrt(jnp.sqrt(jnp.sum(second * second, keepdims=True)))
    scale_out[...] = clip_ratio[...] * (math.sqrt(M) + math.sqrt(N)) / sigma
    basis_out[...] = full_dot(right[...], inverse_factor(second), ((1,), (1,)))
    out_copy.wait()


def power(partial, clip_ratio, start):
    vm = lambda *shape: pltpu.VMEM(shape, F32)
    its = ITERS + 1
    return pl.pallas_call(
        kernel,
        out_shape=(
            jax.ShapeDtypeStruct((TC, K), F32),
            jax.ShapeDtypeStruct((1, 1), F32),
            jax.ShapeDtypeStruct((ROWS, HALF), F32),
        ),
        in_specs=[
            pl.BlockSpec(memory_space=pl.ANY),
            pl.BlockSpec(memory_space=pltpu.VMEM),
            pl.BlockSpec(memory_space=pl.ANY),
        ],
        out_specs=[pl.BlockSpec(memory_space=pltpu.VMEM)] * 2 + [pl.BlockSpec(memory_space=pl.ANY)],
        scratch_shapes=[
            vm(ROWS, HALF),
            vm(ROWS, HALF),
            vm(ROWS, HALF),
            vm(TR, TC),
            pltpu.SemaphoreType.DMA((2 * CHUNKS,)),
            pltpu.SemaphoreType.DMA((2 * CHUNKS,)),
            pltpu.SemaphoreType.DMA((CHUNKS,)),
            pltpu.SemaphoreType.DMA,
            pltpu.SemaphoreType.DMA((CHUNKS,)),
            pltpu.SemaphoreType.DMA((CHUNKS,)),
            pltpu.SemaphoreType.DMA((3,)),
            vm(TC, K),
            vm(ZB, K),
            pltpu.VMEM((TR, TC), BF),
            pltpu.VMEM((TR, TC), BF),
            pltpu.VMEM((TC, TR), BF),
            pltpu.VMEM((TC, TR), BF),
            vm(TC, K),
            pltpu.VMEM((TC, 2 * K), BF),
            vm(TR, K),
            vm(TR, K),
            vm(its, TR // 2, K),
            vm(its, 4, TR // 8, K),
            vm(its, 4, TR // 8, K),
            vm(TR, K),
            vm(TC, K),
            vm(its, 8, ZB, K),
            vm(K, K),
            vm(its, 8, 8, K),
            vm(K, K),
            vm(K, K),
            vm(its, K // 2, K),
            vm(its, 4, K // 2, K),
            vm(its, 4, K // 2, K),
            vm(K, K),
            vm(K, K),
            pltpu.SemaphoreType.DMA((its, SEMS)),
            pltpu.SemaphoreType.DMA((its, SEMS)),
        ],
        compiler_params=pltpu.CompilerParams(
            collective_id=0, has_side_effects=True, vmem_limit_bytes=60 * 2**20
        ),
        name="power",
    )(partial, clip_ratio, start)


def body(partials, clip_ratio, start_block):
    vectors, scale, summed = power(partials[0], clip_ratio.reshape(1, 1), start_block)
    update = summed * scale
    return (update, vectors)


def solution(mesh):
    placed = (P("dp", ("row", "col"), None), P(), P(("dp", "col"), None))
    return jax.shard_map(
        body,
        mesh=mesh,
        in_specs=placed,
        out_specs=(P(("row", "col"), "dp"), P(("dp", "col"), None)),
        check_vma=False,
    )
```

```python
import math

import jax
import jax.numpy as jnp
from jax import lax
from jax.experimental import pallas as pl
from jax.experimental.pallas import tpu as pltpu
from jax.sharding import PartitionSpec as P

M = 8192
N = 28672
K = 128
ITERS = 3
TR = 1024
TC = 896
ROWS = 64
HALF = N // 2
CHUNKS = 8
PANEL = 16
START_AT = 4
WINDOW = 2
ZB = 112
MESH = pl.DeviceIdType.MESH
BF = jnp.bfloat16
F32 = jnp.float32

G2_CORE, G2_X, G2_Y, G2_CG = 0, 1, 5, 9
L_CORE, L_X, L_Y, L_XG, L_CG = 10, 11, 15, 19, 23
G1_RS, G1_AG, G1_CG, W_RS, W_AG = 24, 32, 40, 41, 49
SEMS = 57


def split2(a):
    hi = a.astype(BF)
    return hi, (a - hi.astype(F32)).astype(BF)


def dot_f32(a, b, dims):
    return lax.dot_general(a, b, (dims, ((), ())), preferred_element_type=F32)


def wide(a):
    hi, lo = split2(a)
    return jnp.concatenate([hi, lo], axis=1)


def full_dot(a, b, dims):
    return lax.dot_general(
        a, b, (dims, ((), ())), precision=lax.Precision.HIGHEST, preferred_element_type=F32
    )


def split_product(hi, lo, both):
    first = jnp.dot(hi, both, preferred_element_type=F32)
    return first[:, :K] + first[:, K:] + jnp.dot(lo, both[:, :K], preferred_element_type=F32)


def inverse_factor(gram):
    lane = lax.broadcasted_iota(jnp.int32, (PANEL, K), 1)
    sub = lax.broadcasted_iota(jnp.int32, (PANEL, K), 0)
    col = lax.broadcasted_iota(jnp.int32, (K, K), 1)
    row = lax.broadcasted_iota(jnp.int32, (K, K), 0)

    def split3(a):
        hi = a.astype(BF).astype(F32)
        mid = (a - hi).astype(BF).astype(F32)
        return hi, mid, a - hi - mid

    def step(k, x):
        p = x[0:PANEL, :]
        cols = [jnp.broadcast_to(p[:, i : i + 1], (PANEL, K)) for i in range(PANEL)]
        pivots = []
        for j in range(PANEL):
            heads = [cols[i][j : j + 1, :] for i in range(j, PANEL)]
            pivots.append(heads[0])
            m = jnp.where(sub > j, cols[j] * (1.0 / heads[0]), 0.0)
            for i in range(j + 1, PANEL):
                cols[i] = cols[i] - m * heads[i - j]
            head = jnp.where(lane[:1] == j, 1.0, p[j : j + 1, :])
            p = jnp.where((lane == j) & (sub > j), 0.0, p) - m * head
        pivot = jnp.concatenate(pivots, axis=0)
        rs = lax.rsqrt(pivot)
        rs = rs * (1.5 - 0.5 * pivot * rs * rs)
        p = jnp.where(lane == sub, 1.0, p) * rs
        y = jnp.where((lane < PANEL) & (lane > sub), 0.0, p)
        lead = jnp.where((lane >= PANEL) & (lane < K - PANEL * k), p, 0.0)
        lh, lm, ll = split3(lead)
        yh, ym, yl = split3(y)
        a = jnp.concatenate([lh, lh, lm, lh, ll, lm], axis=0).astype(BF)
        b = jnp.concatenate([yh, ym, yh, yl, yh, ym], axis=0).astype(BF)
        new = jnp.where(col < PANEL, 0.0, x) - dot_f32(a, b, ((0,), (0,)))
        new = jnp.where(row < K - PANEL * k, new, x)
        return pltpu.roll(jnp.concatenate([new[PANEL:, :], y], axis=0), K - PANEL, axis=1)

    x = lax.fori_loop(0, K // PANEL, step, gram)
    return jnp.where(col <= row, x, 0.0)


def kernel(
    partial,
    start,
    right_out,
    second_out,
    summed_out,
    own,
    theirs,
    summed,
    tile,
    dp_send,
    dp_recv,
    own_sem,
    out_sem,
    tile_send,
    tile_recv,
    start_sem,
    moved,
    mine,
    thi,
    tlo,
    thit,
    tlot,
    right,
    rwide,
    left,
    lpart,
    lcore,
    lx,
    ly,
    lsum,
    wpart,
    wz,
    gram1,
    g1z,
    g1share,
    gram2,
    g2core,
    g2x,
    g2y,
    g2sum,
    factor,
    send,
    recv,
):
    d = lax.axis_index("dp")
    z = lax.axis_index("row")
    c = lax.axis_index("col")
    co = lax.rem(c, 2)
    yl = lax.rem(lax.div(c, 2), 2)
    x = lax.div(c, 4)
    zl = lax.rem(z, 2)
    zh = lax.div(z, 2)
    y = d * 2 + zl
    p = yl * 4 + zh
    j = x * 4 + zl * 2 + co

    def dev_core():
        return (d, z, c + 1 - 2 * co)

    def dev_x(i):
        return (d, z, i * 4 + yl * 2 + co)

    def dev_y(i):
        return (lax.div(i, 2), zh * 2 + lax.rem(i, 2), c)

    def dev_p(i):
        return (d, lax.rem(i, 4) * 2 + zl, x * 4 + lax.div(i, 4) * 2 + co)

    def dev_j(i):
        return (d, zh * 2 + lax.rem(lax.div(i, 2), 2), lax.div(i, 4) * 4 + yl * 2 + lax.rem(i, 2))

    partner = (1 - d, z, c)
    across = (d, z, x * 4 + (1 - yl) * 2 + co)

    def dev_end_y(i):
        return (lax.div(i, 2), z, x * 4 + lax.rem(i, 2) * 2 + co)

    def dev_yz(i):
        return (d, lax.rem(i, 8), x * 4 + lax.div(i, 8) * 2 + co)

    barrier = pltpu.get_barrier_semaphore()
    peers = [dev_y(lax.rem(y + o, 4)) for o in (1, 3, 2)]
    peers += [dev_end_y(lax.rem(d * 2 + yl + o, 4)) for o in (1, 3, 2)]
    peers += [dev_yz(lax.rem(yl * 8 + z + o, 16)) for o in range(1, 16)]
    peers += [dev_j(lax.rem(j + o, 16)) for o in range(1, 16)]
    for dev in peers:
        pl.semaphore_signal(barrier, inc=1, device_id=dev, device_id_type=MESH)

    def part_of(k, h, base):
        rows = pl.ds(pl.multiple_of(k * 8, 8), 8)
        return rows, pl.ds(pl.multiple_of(base + h * (HALF // 2), 128), HALF // 2)

    def own_copy(k):
        rows = pl.ds(pl.multiple_of(k * 8, 8), 8)
        mine = pl.ds(pl.multiple_of(d * HALF, HALF), HALF)
        return pltpu.make_async_copy(partial.at[rows, mine], own.at[rows, :], own_sem.at[k])

    def dp_copy(k, turn):
        h = lax.rem(turn + lax.div(x, 2), 2)
        rows, other = part_of(k, h, (1 - d) * HALF)
        return pltpu.make_async_remote_copy(
            src_ref=partial.at[rows, other],
            dst_ref=theirs.at[rows, part_of(k, h, 0)[1]],
            send_sem=dp_send.at[2 * k + turn],
            recv_sem=dp_recv.at[2 * k + turn],
            device_id=partner,
            device_id_type=MESH,
        )

    start_here = pltpu.make_async_copy(start, right, start_sem.at[0])

    def quarter(i):
        return pl.ds(pl.multiple_of(i * (TC // 4), 8), TC // 4)

    def start_copy(src, i, out, into, dev):
        return pltpu.make_async_remote_copy(
            src_ref=src.at[quarter(i), :],
            dst_ref=right.at[quarter(i), :],
            send_sem=start_sem.at[out],
            recv_sem=start_sem.at[into],
            device_id=dev,
            device_id_type=MESH,
        )

    start_across = start_copy(start, zh, 1, 2, across)

    def start_relay(o):
        return start_copy(right, zh, 2 + o, 5 + o, (d, lax.rem(zh + o, 4) * 2 + zl, c))

    def start_relayed(o):
        return start_copy(right, lax.rem(zh + 4 - o, 4), 2 + o, 5 + o, across)

    for k in range(CHUNKS):
        own_copy(k).start()
    pl.semaphore_wait(barrier, len(peers))

    @pl.when(yl == zl)
    def _():
        start_across.start()
        start_here.start()

    for k in range(WINDOW):
        dp_copy(k, 0).start()
        dp_copy(k, 1).start()

    def prepare(k):
        rows = pl.ds(pl.multiple_of(k * 128, 128), 128)
        got = tile.at[pl.ds(0, 120), :]
        pltpu.make_async_copy(got, got, tile_recv.at[k]).wait()
        part = tile[rows, :]
        hi, lo = split2(part)
        thi[rows, :] = hi
        tlo[rows, :] = lo
        hi, lo = split2(part.T)
        thit[:, rows] = hi
        tlot[:, rows] = lo

    def first_product(k):
        rows = pl.ds(pl.multiple_of(k * 128, 128), 128)
        lpart[rows, :] = split_product(thi[rows, :], tlo[rows, :], rwide[...])

    def chunk(k, carry):
        rows = pl.ds(pl.multiple_of(k * 8, 8), 8)
        place = pl.ds(pl.multiple_of(k * 128 + j * 8, 8), 8)
        own_copy(k).wait()
        for turn in (0, 1):
            dp_copy(k, turn).wait()

            @pl.when(k + WINDOW < CHUNKS)
            def _():
                dp_copy(k + WINDOW, turn).start()

            h = lax.rem(turn + lax.div(x, 2), 2)
            half = part_of(k, h, 0)[1]
            summed[rows, half] = own[rows, half] + theirs[rows, half]

            def block(i):
                return summed.at[rows, pl.ds(pl.multiple_of(i * TC, 128), TC)]

            def send_block(o):
                i = h * 8 + lax.rem(j + o, 8)
                pltpu.make_async_remote_copy(
                    src_ref=block(i),
                    dst_ref=tile.at[place, :],
                    send_sem=tile_send.at[k],
                    recv_sem=tile_recv.at[k],
                    device_id=dev_j(i),
                    device_id_type=MESH,
                ).start()

            if turn == 0:
                tile[place, :] = block(j)[...]
            else:
                send_block(0)
            for o in range(1, 8):
                send_block(o)

        @pl.when((k == 0) & (yl != zl))
        def _():
            start_across.wait_recv()
            for o in (1, 3, 2):
                start_relay(o).start()

        @pl.when(k == START_AT)
        def _():
            @pl.when(yl == zl)
            def _():
                start_here.wait()
                start_across.wait_send()

            @pl.when(yl != zl)
            def _():
                for o in (1, 3, 2):
                    start_relay(o).wait_send()
                    start_relayed(o).wait_recv()

            right[...] = right[...] * math.sqrt(3.0 / N)
            rwide[...] = wide(right[...])
            for i in range(START_AT - 1):
                first_product(i)

        @pl.when(k > 0)
        def _():
            prepare(k - 1)

        @pl.when(k >= START_AT)
        def _():
            first_product(k - 1)

        return carry

    lax.fori_loop(0, CHUNKS, chunk, 0)
    out_copy = pltpu.make_async_copy(summed, summed_out, out_sem)
    out_copy.start()
    prepare(CHUNKS - 1)
    first_product(CHUNKS - 1)
    for k in range(CHUNKS):
        sent = tile.at[pl.ds(0, 120), :]
        pltpu.make_async_copy(sent, sent, tile_send.at[k]).wait()

    def copy(src, dst, it, slot_out, slot_in, dev):
        return pltpu.make_async_remote_copy(
            src_ref=src,
            dst_ref=dst,
            send_sem=send.at[it, slot_out],
            recv_sem=recv.at[it, slot_in],
            device_id=dev,
            device_id_type=MESH,
        )

    def ring(n, me, dev, base, it, src, dst):
        for o in sorted(range(1, n), key=lambda o: min(o, n - o)):
            i = lax.rem(me + o, n)
            copy(src(i), dst(me), it, base + o, base + o, dev(i)).start()

    def ring_wait(n, me, dev, base, it, src, dst):
        for o in sorted(range(1, n), key=lambda o: min(o, n - o)):
            i = lax.rem(me + n - o, n)
            copy(src(i), dst(i), it, base + o, base + o, dev(i)).wait()

    def blocks_at(i, size):
        return pl.ds(pl.multiple_of(i * size, 8), size)

    def blocks(ref, size):
        return lambda i: ref.at[pl.ds(pl.multiple_of(i * size, size), size), :]

    class Plane:
        def __init__(self, it, rows, part, core_buf, x_buf, y_buf, total, sems, y, dev_y):
            self.it, self.rows, self.y, self.dev_y = it, rows, y, dev_y
            self.part, self.core_buf, self.x_buf, self.y_buf, self.total = part, core_buf, x_buf, y_buf, total
            self.s_core, self.s_x, self.s_y, self.s_xg, self.s_cg = sems
            self.half, self.unit = rows // 2, rows // 8

        def mine(self):
            return pl.ds(pl.multiple_of(co * self.half + x * self.unit, self.unit), self.unit)

        def core_copy(self):
            there = pl.ds(pl.multiple_of((1 - co) * self.half, self.half), self.half)
            return copy(self.part.at[there, :], self.core_buf.at[self.it], self.it, self.s_core, self.s_core, dev_core())

        def core_done(self):
            self.core_copy().wait()
            here = pl.ds(pl.multiple_of(co * self.half, self.half), self.half)
            self.core_buf[self.it] = self.core_buf[self.it] + self.part[here, :]

        def x_args(self):
            src = lambda i: self.core_buf.at[self.it, pl.ds(pl.multiple_of(i * self.unit, self.unit), self.unit), :]
            return (4, x, dev_x, self.s_x, self.it, src, lambda i: self.x_buf.at[self.it, i])

        def x_send(self):
            own = self.core_buf[self.it, pl.ds(pl.multiple_of(x * self.unit, self.unit), self.unit), :]
            self.x_buf[self.it, x] = own
            ring(*self.x_args())

        def x_done(self):
            ring_wait(*self.x_args())
            self.y_buf[self.it, self.y] = (self.x_buf[self.it, 0] + self.x_buf[self.it, 1]) + (
                self.x_buf[self.it, 2] + self.x_buf[self.it, 3]
            )

        def y_args(self):
            return (
                4,
                self.y,
                self.dev_y,
                self.s_y,
                self.it,
                lambda i: self.y_buf.at[self.it, self.y],
                lambda i: self.y_buf.at[self.it, i],
            )

        def y_send(self):
            ring(*self.y_args())

        def y_done(self):
            ring_wait(*self.y_args())
            self.total[self.mine(), :] = (self.y_buf[self.it, 0] + self.y_buf[self.it, 1]) + (
                self.y_buf[self.it, 2] + self.y_buf[self.it, 3]
            )

        def xg_args(self):
            place = lambda i: self.total.at[pl.ds(pl.multiple_of(co * self.half + i * self.unit, self.unit), self.unit), :]
            return (4, x, dev_x, self.s_xg, self.it, lambda i: place(x), place)

        def xg_send(self):
            ring(*self.xg_args())

        def xg_done(self):
            ring_wait(*self.xg_args())

        def cg_copy(self):
            here = self.total.at[pl.ds(pl.multiple_of(co * self.half, self.half), self.half), :]
            return copy(here, here, self.it, self.s_cg, self.s_cg, dev_core())

    class Small(Plane):
        def mine(self):
            return pl.ds(pl.multiple_of(co * self.half, self.half), self.half)

        def x_args(self):
            return (4, x, dev_x, self.s_x, self.it, lambda i: self.x_buf.at[self.it, x], lambda i: self.x_buf.at[self.it, i])

        def x_send(self):
            self.x_buf[self.it, x] = self.core_buf[self.it]
            ring(*self.x_args())

    def left_plane(it):
        return Plane(it, TR, lpart, lcore, lx, ly, lsum, (L_CORE, L_X, L_Y, L_XG, L_CG), y, dev_y)

    def second_plane(it, y=y, dev_y=dev_y):
        return Small(it, K, gram2, g2core, g2x, g2y, g2sum, (G2_CORE, G2_X, G2_Y, None, G2_CG), y, dev_y)

    def iteration(it, carry):
        lp, sp = left_plane(it), second_plane(it)

        @pl.when(it > 0)
        def _():
            gram2[...] = full_dot(right[...], right[...], ((0,), (0,)))
            sp.core_copy().start()

        for half in (1 - co, co):
            rows = pl.ds(pl.multiple_of(half * (TR // 2), TR // 2), TR // 2)

            @pl.when(it > 0)
            def _(rows=rows):
                lpart[rows, :] = split_product(thi[rows, :], tlo[rows, :], rwide[...])

            if half is not co:
                lp.core_copy().start()

        @pl.when(it > 0)
        def _():
            sp.core_done()
            sp.x_send()

        lp.core_done()
        lp.x_send()

        @pl.when(it > 0)
        def _():
            sp.x_done()
            sp.y_send()

        lp.x_done()
        lp.y_send()

        @pl.when(it > 0)
        def _():
            sp.y_done()
            sp.cg_copy().start()

        lp.y_done()
        lp.xg_send()

        lp.xg_done()
        lp.cg_copy().start()

        @pl.when(it > 0)
        def _():
            sp.cg_copy().wait()
            factor[...] = inverse_factor(g2sum[...])

        lp.cg_copy().wait()

        @pl.when(it == 0)
        def _():
            left[...] = lsum[...]

        @pl.when(it > 0)
        def _():
            left[...] = full_dot(lsum[...], factor[...], ((1,), (1,)))

        gram1[...] = full_dot(left[...], left[...], ((0,), (0,)))
        half = pl.ds(pl.multiple_of(co * (K // 2), K // 2), K // 2)
        part = gram1.at[half, :]
        g1_rs = (8, p, dev_p, G1_RS, it, blocks(part, 8), lambda i: g1z.at[it, i])
        g1z[it, p] = gram1[pl.ds(pl.multiple_of(co * (K // 2) + p * 8, 8), 8), :]
        ring(*g1_rs)

        lwide = wide(left[...])
        w_rs = (8, p, dev_p, W_RS, it, blocks(wpart, ZB), lambda i: wz.at[it, i])
        for turn in (0, 1):
            h = lax.rem(yl + turn, 2)
            rows = pl.ds(pl.multiple_of(h * (TC // 2), TC // 2), TC // 2)
            wpart[rows, :] = split_product(thit[rows, :], tlot[rows, :], lwide)
            if turn == 0:
                wz[it, p] = wpart[pl.ds(pl.multiple_of(p * ZB, 16), ZB), :]
            for o in (0, 1, 3, 2)[1 - turn :]:
                i = h * 4 + lax.rem(zh + o, 4)
                far = lax.rem(i + 8 - p, 8)
                copy(wpart.at[blocks_at(i, ZB), :], wz.at[it, p], it, W_RS + far, W_RS + far, dev_p(i)).start()

        ring_wait(*g1_rs)
        total = g1z[it, 0]
        for i in range(1, 8):
            total = total + g1z[it, i]
        g1share[pl.ds(pl.multiple_of(co * (K // 2) + p * 8, 8), 8), :] = total
        share = blocks(g1share.at[half, :], 8)
        g1_ag = (8, p, dev_p, G1_AG, it, lambda i: share(p), share)
        ring(*g1_ag)

        ring_wait(*w_rs)
        total = wz[it, 0]
        for i in range(1, 8):
            total = total + wz[it, i]

        place = blocks(right, ZB)
        w_ag = (8, p, dev_p, W_AG, it, lambda i: place(p), place)
        end_place = blocks(moved, ZB)

        def end_send(i):
            return copy(mine, end_place(p), it, W_AG + i, W_AG + p, (d, i, x * 4 + zl * 2 + co))

        def end_recv(i):
            sender = (d, lax.rem(i, 4) * 2 + yl, x * 4 + lax.div(i, 4) * 2 + co)
            return copy(mine, end_place(i), it, W_AG + i, W_AG + i, sender)

        @pl.when(it < ITERS - 1)
        def _():
            right[blocks_at(p, ZB), :] = total
            ring(*w_ag)

        @pl.when(it == ITERS - 1)
        def _():
            mine[...] = total
            for i in range(8):

                @pl.when((i != z) | (yl != zl))
                def _(i=i):
                    end_send(i).start()

            @pl.when(yl == zl)
            def _():
                moved[blocks_at(p, ZB), :] = total

        ring_wait(*g1_ag)
        swap = copy(g1share.at[half, :], g1share.at[half, :], it, G1_CG, G1_CG, dev_core())
        swap.start()
        swap.wait()
        factor[...] = inverse_factor(g1share[...])

        @pl.when(it < ITERS - 1)
        def _():
            ring_wait(*w_ag)
            right[...] = full_dot(right[...], factor[...], ((1,), (1,)))

        @pl.when(it == ITERS - 1)
        def _():
            for i in range(8):

                @pl.when((i != z) | (yl != zl))
                def _(i=i):
                    end_send(i).wait_send()

                @pl.when((i != p) | (yl != zl))
                def _(i=i):
                    end_recv(i).wait_recv()

            right[...] = full_dot(moved[...], factor[...], ((1,), (1,)))

        rwide[...] = wide(right[...])
        return carry

    lax.fori_loop(0, ITERS, iteration, 0)

    sp = second_plane(ITERS, d * 2 + yl, dev_end_y)
    gram2[...] = full_dot(right[...], right[...], ((0,), (0,)))
    sp.core_copy().start()
    sp.core_done()
    sp.x_send()
    sp.x_done()
    sp.y_send()
    sp.y_done()
    sp.cg_copy().start()
    sp.cg_copy().wait()
    second_out[...] = g2sum[...]
    right_out[...] = right[...]
    out_copy.wait()


def power(partial, start):
    vm = lambda *shape: pltpu.VMEM(shape, F32)
    its = ITERS + 1
    return pl.pallas_call(
        kernel,
        out_shape=(
            jax.ShapeDtypeStruct((TC, K), F32),
            jax.ShapeDtypeStruct((K, K), F32),
            jax.ShapeDtypeStruct((ROWS, HALF), F32),
        ),
        in_specs=[
            pl.BlockSpec(memory_space=pl.ANY),
            pl.BlockSpec(memory_space=pl.ANY),
        ],
        out_specs=[pl.BlockSpec(memory_space=pltpu.VMEM)] * 2 + [pl.BlockSpec(memory_space=pl.ANY)],
        scratch_shapes=[
            vm(ROWS, HALF),
            vm(ROWS, HALF),
            vm(ROWS, HALF),
            vm(TR, TC),
            pltpu.SemaphoreType.DMA((2 * CHUNKS,)),
            pltpu.SemaphoreType.DMA((2 * CHUNKS,)),
            pltpu.SemaphoreType.DMA((CHUNKS,)),
            pltpu.SemaphoreType.DMA,
            pltpu.SemaphoreType.DMA((CHUNKS,)),
            pltpu.SemaphoreType.DMA((CHUNKS,)),
            pltpu.SemaphoreType.DMA((9,)),
            vm(TC, K),
            vm(ZB, K),
            pltpu.VMEM((TR, TC), BF),
            pltpu.VMEM((TR, TC), BF),
            pltpu.VMEM((TC, TR), BF),
            pltpu.VMEM((TC, TR), BF),
            vm(TC, K),
            pltpu.VMEM((TC, 2 * K), BF),
            vm(TR, K),
            vm(TR, K),
            vm(its, TR // 2, K),
            vm(its, 4, TR // 8, K),
            vm(its, 4, TR // 8, K),
            vm(TR, K),
            vm(TC, K),
            vm(its, 8, ZB, K),
            vm(K, K),
            vm(its, 8, 8, K),
            vm(K, K),
            vm(K, K),
            vm(its, K // 2, K),
            vm(its, 4, K // 2, K),
            vm(its, 4, K // 2, K),
            vm(K, K),
            vm(K, K),
            pltpu.SemaphoreType.DMA((its, SEMS)),
            pltpu.SemaphoreType.DMA((its, SEMS)),
        ],
        compiler_params=pltpu.CompilerParams(
            collective_id=0, has_side_effects=True, vmem_limit_bytes=60 * 2**20
        ),
        name="power",
    )(partial, start)


def finish_kernel(summed, right, second, clip_ratio, update_out, basis_out, block, vectors, in_sem, out_sem, right_sem):
    def into(k):
        return pltpu.make_async_copy(summed.at[pl.ds(k * 8, 8), :], block.at[pl.ds(k * 8, 8), :], in_sem.at[k])

    def out(k):
        return pltpu.make_async_copy(block.at[pl.ds(k * 8, 8), :], update_out.at[pl.ds(k * 8, 8), :], out_sem.at[k])

    right_copy = pltpu.make_async_copy(right, vectors, right_sem)
    for k in range(CHUNKS):
        into(k).start()
    right_copy.start()
    sigma = jnp.sqrt(jnp.sqrt(jnp.sum(second[...] * second[...], keepdims=True)))
    scale = clip_ratio[...] * (math.sqrt(M) + math.sqrt(N)) / sigma
    for k in range(CHUNKS):
        into(k).wait()
        block[k * 8 : (k + 1) * 8, :] = block[k * 8 : (k + 1) * 8, :] * scale
        out(k).start()
    factor = inverse_factor(second[...])
    right_copy.wait()
    basis_out[...] = full_dot(vectors[...], factor, ((1,), (1,)))
    for k in range(CHUNKS):
        out(k).wait()


def finish(summed, right, second, clip_ratio):
    return pl.pallas_call(
        finish_kernel,
        out_shape=(jax.ShapeDtypeStruct((ROWS, HALF), F32), jax.ShapeDtypeStruct((TC, K), F32)),
        in_specs=[pl.BlockSpec(memory_space=pl.ANY)] * 2 + [pl.BlockSpec(memory_space=pltpu.VMEM)] * 2,
        out_specs=(pl.BlockSpec(memory_space=pl.ANY), pl.BlockSpec(memory_space=pltpu.VMEM)),
        scratch_shapes=[
            pltpu.VMEM((ROWS, HALF), F32),
            pltpu.VMEM((TC, K), F32),
            pltpu.SemaphoreType.DMA((CHUNKS,)),
            pltpu.SemaphoreType.DMA((CHUNKS,)),
            pltpu.SemaphoreType.DMA,
        ],
        compiler_params=pltpu.CompilerParams(vmem_limit_bytes=60 * 2**20),
        name="finish",
    )(summed, right, second, clip_ratio)


def body(partials, clip_ratio, start_block):
    right, second, summed = power(partials[0], start_block)
    return finish(summed, right, second, clip_ratio.reshape(1, 1))


def solution(mesh):
    placed = (P("dp", ("row", "col"), None), P(), P(("dp", "col"), None))
    return jax.shard_map(
        body,
        mesh=mesh,
        in_specs=placed,
        out_specs=(P(("row", "col"), "dp"), P(("dp", "col"), None)),
        check_vma=False,
    )
```

```python
import math

import jax
import jax.numpy as jnp
from jax import lax
from jax.experimental import pallas as pl
from jax.experimental.pallas import tpu as pltpu
from jax.sharding import PartitionSpec as P

M = 8192
N = 28672
K = 128
ITERS = 3
TR = 1024
TC = 896
ROWS = 64
HALF = N // 2
CHUNKS = 8
PANEL = 16
START_AT = 4
WINDOW = 2
ZB = 112
MESH = pl.DeviceIdType.MESH
FAR_FIRST = {4: (2, 1, 3), 8: (6, 2, 5, 7, 1, 3, 4)}
BF = jnp.bfloat16
F32 = jnp.float32

G2_CORE, G2_X, G2_Y, G2_CG = 0, 1, 5, 9
L_CORE, L_X, L_Y, L_XG, L_CG = 10, 11, 15, 19, 23
G1_RS, G1_AG, G1_CG, W_RS, W_AG = 24, 32, 40, 41, 49
SEMS = 57


def split2(a):
    hi = a.astype(BF)
    return hi, (a - hi.astype(F32)).astype(BF)


def dot_f32(a, b, dims):
    return lax.dot_general(a, b, (dims, ((), ())), preferred_element_type=F32)


def wide(a):
    hi, lo = split2(a)
    return jnp.concatenate([hi, lo], axis=1)


def full_dot(a, b, dims):
    return lax.dot_general(
        a, b, (dims, ((), ())), precision=lax.Precision.HIGHEST, preferred_element_type=F32
    )


def split_product(hi, lo, both):
    first = jnp.dot(hi, both, preferred_element_type=F32)
    return first[:, :K] + first[:, K:] + jnp.dot(lo, both[:, :K], preferred_element_type=F32)


def inverse_factor(gram):
    lane = lax.broadcasted_iota(jnp.int32, (PANEL, K), 1)
    sub = lax.broadcasted_iota(jnp.int32, (PANEL, K), 0)
    col = lax.broadcasted_iota(jnp.int32, (K, K), 1)
    row = lax.broadcasted_iota(jnp.int32, (K, K), 0)

    def split3(a):
        hi = a.astype(BF).astype(F32)
        mid = (a - hi).astype(BF).astype(F32)
        return hi, mid, a - hi - mid

    def step(k, x):
        p = x[0:PANEL, :]
        cols = [jnp.broadcast_to(p[:, i : i + 1], (PANEL, K)) for i in range(PANEL)]
        pivots = []
        for j in range(PANEL):
            heads = [cols[i][j : j + 1, :] for i in range(j, PANEL)]
            pivots.append(heads[0])
            m = jnp.where(sub > j, cols[j] * (1.0 / heads[0]), 0.0)
            for i in range(j + 1, PANEL):
                cols[i] = cols[i] - m * heads[i - j]
            head = jnp.where(lane[:1] == j, 1.0, p[j : j + 1, :])
            p = jnp.where((lane == j) & (sub > j), 0.0, p) - m * head
        pivot = jnp.concatenate(pivots, axis=0)
        rs = lax.rsqrt(pivot)
        rs = rs * (1.5 - 0.5 * pivot * rs * rs)
        p = jnp.where(lane == sub, 1.0, p) * rs
        y = jnp.where((lane < PANEL) & (lane > sub), 0.0, p)
        lead = jnp.where((lane >= PANEL) & (lane < K - PANEL * k), p, 0.0)
        lh, lm, ll = split3(lead)
        yh, ym, yl = split3(y)
        a = jnp.concatenate([lh, lh, lm, lh, ll, lm], axis=0).astype(BF)
        b = jnp.concatenate([yh, ym, yh, yl, yh, ym], axis=0).astype(BF)
        new = jnp.where(col < PANEL, 0.0, x) - dot_f32(a, b, ((0,), (0,)))
        new = jnp.where(row < K - PANEL * k, new, x)
        return pltpu.roll(jnp.concatenate([new[PANEL:, :], y], axis=0), K - PANEL, axis=1)

    x = lax.fori_loop(0, K // PANEL, step, gram)
    return jnp.where(col <= row, x, 0.0)


def kernel(
    partial,
    start,
    right_out,
    second_out,
    summed_out,
    own,
    theirs,
    summed,
    tile,
    dp_send,
    dp_recv,
    own_sem,
    out_sem,
    tile_send,
    tile_recv,
    start_sem,
    moved,
    mine,
    thi,
    tlo,
    thit,
    tlot,
    right,
    rwide,
    left,
    lpart,
    lcore,
    lx,
    ly,
    lsum,
    wpart,
    wz,
    gram1,
    g1z,
    g1share,
    gram2,
    g2core,
    g2x,
    g2y,
    g2sum,
    factor,
    send,
    recv,
):
    d = lax.axis_index("dp")
    z = lax.axis_index("row")
    c = lax.axis_index("col")
    co = lax.rem(c, 2)
    yl = lax.rem(lax.div(c, 2), 2)
    x = lax.div(c, 4)
    zl = lax.rem(z, 2)
    zh = lax.div(z, 2)
    y = d * 2 + zl
    p = yl * 4 + zh
    j = x * 4 + zl * 2 + co

    def dev_core():
        return (d, z, c + 1 - 2 * co)

    def dev_x(i):
        return (d, z, i * 4 + yl * 2 + co)

    def dev_y(i):
        return (lax.div(i, 2), zh * 2 + lax.rem(i, 2), c)

    def dev_p(i):
        return (d, lax.rem(i, 4) * 2 + zl, x * 4 + lax.div(i, 4) * 2 + co)

    def dev_j(i):
        return (d, zh * 2 + lax.rem(lax.div(i, 2), 2), lax.div(i, 4) * 4 + yl * 2 + lax.rem(i, 2))

    partner = (1 - d, z, c)
    across = (d, z, x * 4 + (1 - yl) * 2 + co)

    def dev_end_y(i):
        return (lax.div(i, 2), z, x * 4 + lax.rem(i, 2) * 2 + co)

    def dev_yz(i):
        return (d, lax.rem(i, 8), x * 4 + lax.div(i, 8) * 2 + co)

    barrier = pltpu.get_barrier_semaphore()
    peers = [dev_y(lax.rem(y + o, 4)) for o in (1, 3, 2)]
    peers += [dev_end_y(lax.rem(d * 2 + yl + o, 4)) for o in (1, 3, 2)]
    peers += [dev_yz(lax.rem(yl * 8 + z + o, 16)) for o in range(1, 16)]
    peers += [dev_j(lax.rem(j + o, 16)) for o in range(1, 16)]
    for dev in peers:
        pl.semaphore_signal(barrier, inc=1, device_id=dev, device_id_type=MESH)

    def part_of(k, h, base):
        rows = pl.ds(pl.multiple_of(k * 8, 8), 8)
        return rows, pl.ds(pl.multiple_of(base + h * (HALF // 2), 128), HALF // 2)

    def own_copy(k):
        rows = pl.ds(pl.multiple_of(k * 8, 8), 8)
        mine = pl.ds(pl.multiple_of(d * HALF, HALF), HALF)
        return pltpu.make_async_copy(partial.at[rows, mine], own.at[rows, :], own_sem.at[k])

    def dp_copy(k, turn):
        h = lax.rem(turn + lax.div(x, 2), 2)
        rows, other = part_of(k, h, (1 - d) * HALF)
        return pltpu.make_async_remote_copy(
            src_ref=partial.at[rows, other],
            dst_ref=theirs.at[rows, part_of(k, h, 0)[1]],
            send_sem=dp_send.at[2 * k + turn],
            recv_sem=dp_recv.at[2 * k + turn],
            device_id=partner,
            device_id_type=MESH,
        )

    start_here = pltpu.make_async_copy(start, right, start_sem.at[0])

    def quarter(i):
        return pl.ds(pl.multiple_of(i * (TC // 4), 8), TC // 4)

    def start_copy(src, i, out, into, dev):
        return pltpu.make_async_remote_copy(
            src_ref=src.at[quarter(i), :],
            dst_ref=right.at[quarter(i), :],
            send_sem=start_sem.at[out],
            recv_sem=start_sem.at[into],
            device_id=dev,
            device_id_type=MESH,
        )

    start_across = start_copy(start, zh, 1, 2, across)

    def start_relay(o):
        return start_copy(right, zh, 2 + o, 5 + o, (d, lax.rem(zh + o, 4) * 2 + zl, c))

    def start_relayed(o):
        return start_copy(right, lax.rem(zh + 4 - o, 4), 2 + o, 5 + o, across)

    for k in range(CHUNKS):
        own_copy(k).start()
    pl.semaphore_wait(barrier, len(peers))

    @pl.when(yl == zl)
    def _():
        start_across.start()
        start_here.start()

    for k in range(WINDOW):
        dp_copy(k, 0).start()
        dp_copy(k, 1).start()

    def prepare(k):
        rows = pl.ds(pl.multiple_of(k * 128, 128), 128)
        got = tile.at[pl.ds(0, 120), :]
        pltpu.make_async_copy(got, got, tile_recv.at[k]).wait()
        part = tile[rows, :]
        hi, lo = split2(part)
        thi[rows, :] = hi
        tlo[rows, :] = lo
        hi, lo = split2(part.T)
        thit[:, rows] = hi
        tlot[:, rows] = lo

    def first_product(k):
        rows = pl.ds(pl.multiple_of(k * 128, 128), 128)
        lpart[rows, :] = split_product(thi[rows, :], tlo[rows, :], rwide[...])

    def chunk(k, carry):
        rows = pl.ds(pl.multiple_of(k * 8, 8), 8)
        place = pl.ds(pl.multiple_of(k * 128 + j * 8, 8), 8)
        own_copy(k).wait()
        for turn in (0, 1):
            dp_copy(k, turn).wait()

            @pl.when(k + WINDOW < CHUNKS)
            def _():
                dp_copy(k + WINDOW, turn).start()

            h = lax.rem(turn + lax.div(x, 2), 2)
            half = part_of(k, h, 0)[1]
            summed[rows, half] = own[rows, half] + theirs[rows, half]

            def block(i):
                return summed.at[rows, pl.ds(pl.multiple_of(i * TC, 128), TC)]

            def send_block(o):
                i = h * 8 + lax.rem(j + o, 8)
                pltpu.make_async_remote_copy(
                    src_ref=block(i),
                    dst_ref=tile.at[place, :],
                    send_sem=tile_send.at[k],
                    recv_sem=tile_recv.at[k],
                    device_id=dev_j(i),
                    device_id_type=MESH,
                ).start()

            if turn == 0:
                tile[place, :] = block(j)[...]
            else:
                send_block(0)
            for o in range(1, 8):
                send_block(o)

        @pl.when((k == 0) & (yl != zl))
        def _():
            start_across.wait_recv()
            for o in (1, 3, 2):
                start_relay(o).start()

        @pl.when(k == START_AT)
        def _():
            @pl.when(yl == zl)
            def _():
                start_here.wait()
                start_across.wait_send()

            @pl.when(yl != zl)
            def _():
                for o in (1, 3, 2):
                    start_relay(o).wait_send()
                    start_relayed(o).wait_recv()

            right[...] = right[...] * math.sqrt(3.0 / N)
            rwide[...] = wide(right[...])
            for i in range(START_AT - 1):
                first_product(i)

        @pl.when(k > 0)
        def _():
            prepare(k - 1)

        @pl.when(k >= START_AT)
        def _():
            first_product(k - 1)

        return carry

    lax.fori_loop(0, CHUNKS, chunk, 0)
    out_copy = pltpu.make_async_copy(summed, summed_out, out_sem)
    out_copy.start()
    prepare(CHUNKS - 1)
    first_product(CHUNKS - 1)
    for k in range(CHUNKS):
        sent = tile.at[pl.ds(0, 120), :]
        pltpu.make_async_copy(sent, sent, tile_send.at[k]).wait()

    def copy(src, dst, it, slot_out, slot_in, dev):
        return pltpu.make_async_remote_copy(
            src_ref=src,
            dst_ref=dst,
            send_sem=send.at[it, slot_out],
            recv_sem=recv.at[it, slot_in],
            device_id=dev,
            device_id_type=MESH,
        )

    def ring(n, me, dev, base, it, src, dst):
        for o in FAR_FIRST[n]:
            i = lax.rem(me + o, n)
            copy(src(i), dst(me), it, base + o, base + o, dev(i)).start()

    def ring_wait(n, me, dev, base, it, src, dst):
        for o in FAR_FIRST[n]:
            i = lax.rem(me + n - o, n)
            copy(src(i), dst(i), it, base + o, base + o, dev(i)).wait()

    def blocks_at(i, size):
        return pl.ds(pl.multiple_of(i * size, 8), size)

    def blocks(ref, size):
        return lambda i: ref.at[pl.ds(pl.multiple_of(i * size, size), size), :]

    class Plane:
        def __init__(self, it, rows, part, core_buf, x_buf, y_buf, total, sems, y, dev_y):
            self.it, self.rows, self.y, self.dev_y = it, rows, y, dev_y
            self.part, self.core_buf, self.x_buf, self.y_buf, self.total = part, core_buf, x_buf, y_buf, total
            self.s_core, self.s_x, self.s_y, self.s_xg, self.s_cg = sems
            self.half, self.unit = rows // 2, rows // 8

        def mine(self):
            return pl.ds(pl.multiple_of(co * self.half + x * self.unit, self.unit), self.unit)

        def core_copy(self):
            there = pl.ds(pl.multiple_of((1 - co) * self.half, self.half), self.half)
            return copy(self.part.at[there, :], self.core_buf.at[self.it], self.it, self.s_core, self.s_core, dev_core())

        def core_done(self):
            self.core_copy().wait()
            here = pl.ds(pl.multiple_of(co * self.half, self.half), self.half)
            self.core_buf[self.it] = self.core_buf[self.it] + self.part[here, :]

        def x_args(self):
            src = lambda i: self.core_buf.at[self.it, pl.ds(pl.multiple_of(i * self.unit, self.unit), self.unit), :]
            return (4, x, dev_x, self.s_x, self.it, src, lambda i: self.x_buf.at[self.it, i])

        def x_send(self):
            own = self.core_buf[self.it, pl.ds(pl.multiple_of(x * self.unit, self.unit), self.unit), :]
            self.x_buf[self.it, x] = own
            ring(*self.x_args())

        def x_done(self):
            ring_wait(*self.x_args())
            self.y_buf[self.it, self.y] = (self.x_buf[self.it, 0] + self.x_buf[self.it, 1]) + (
                self.x_buf[self.it, 2] + self.x_buf[self.it, 3]
            )

        def y_args(self):
            return (
                4,
                self.y,
                self.dev_y,
                self.s_y,
                self.it,
                lambda i: self.y_buf.at[self.it, self.y],
                lambda i: self.y_buf.at[self.it, i],
            )

        def y_send(self):
            ring(*self.y_args())

        def y_done(self):
            ring_wait(*self.y_args())
            self.total[self.mine(), :] = (self.y_buf[self.it, 0] + self.y_buf[self.it, 1]) + (
                self.y_buf[self.it, 2] + self.y_buf[self.it, 3]
            )

        def xg_args(self):
            place = lambda i: self.total.at[pl.ds(pl.multiple_of(co * self.half + i * self.unit, self.unit), self.unit), :]
            return (4, x, dev_x, self.s_xg, self.it, lambda i: place(x), place)

        def xg_send(self):
            ring(*self.xg_args())

        def xg_done(self):
            ring_wait(*self.xg_args())

        def cg_copy(self):
            here = self.total.at[pl.ds(pl.multiple_of(co * self.half, self.half), self.half), :]
            return copy(here, here, self.it, self.s_cg, self.s_cg, dev_core())

    class Small(Plane):
        def mine(self):
            return pl.ds(pl.multiple_of(co * self.half, self.half), self.half)

        def x_args(self):
            return (4, x, dev_x, self.s_x, self.it, lambda i: self.x_buf.at[self.it, x], lambda i: self.x_buf.at[self.it, i])

        def x_send(self):
            self.x_buf[self.it, x] = self.core_buf[self.it]
            ring(*self.x_args())

    def left_plane(it):
        return Plane(it, TR, lpart, lcore, lx, ly, lsum, (L_CORE, L_X, L_Y, L_XG, L_CG), y, dev_y)

    def second_plane(it, y=y, dev_y=dev_y):
        return Small(it, K, gram2, g2core, g2x, g2y, g2sum, (G2_CORE, G2_X, G2_Y, None, G2_CG), y, dev_y)

    def iteration(it, carry):
        lp, sp = left_plane(it), second_plane(it)

        @pl.when(it > 0)
        def _():
            gram2[...] = full_dot(right[...], right[...], ((0,), (0,)))
            sp.core_copy().start()

        for half in (1 - co, co):
            rows = pl.ds(pl.multiple_of(half * (TR // 2), TR // 2), TR // 2)

            @pl.when(it > 0)
            def _(rows=rows):
                lpart[rows, :] = split_product(thi[rows, :], tlo[rows, :], rwide[...])

            if half is not co:
                lp.core_copy().start()

        @pl.when(it > 0)
        def _():
            sp.core_done()
            sp.x_send()

        lp.core_done()
        lp.x_send()

        @pl.when(it > 0)
        def _():
            sp.x_done()
            sp.y_send()

        lp.x_done()
        lp.y_send()

        @pl.when(it > 0)
        def _():
            sp.y_done()
            sp.cg_copy().start()

        lp.y_done()
        lp.xg_send()

        @pl.when(it > 0)
        def _():
            sp.cg_copy().wait()
            factor[...] = inverse_factor(g2sum[...])

        lp.xg_done()
        lp.cg_copy().start()
        lp.cg_copy().wait()

        @pl.when(it == 0)
        def _():
            left[...] = lsum[...]

        @pl.when(it > 0)
        def _():
            left[...] = full_dot(lsum[...], factor[...], ((1,), (1,)))

        gram1[...] = full_dot(left[...], left[...], ((0,), (0,)))
        half = pl.ds(pl.multiple_of(co * (K // 2), K // 2), K // 2)
        part = gram1.at[half, :]
        g1_rs = (8, p, dev_p, G1_RS, it, blocks(part, 8), lambda i: g1z.at[it, i])
        g1z[it, p] = gram1[pl.ds(pl.multiple_of(co * (K // 2) + p * 8, 8), 8), :]
        ring(*g1_rs)

        lwide = wide(left[...])
        w_rs = (8, p, dev_p, W_RS, it, blocks(wpart, ZB), lambda i: wz.at[it, i])
        for turn in (0, 1):
            h = lax.rem(yl + 1 - turn, 2)
            rows = pl.ds(pl.multiple_of(h * (TC // 2), TC // 2), TC // 2)
            wpart[rows, :] = split_product(thit[rows, :], tlot[rows, :], lwide)
            if turn == 1:
                wz[it, p] = wpart[pl.ds(pl.multiple_of(p * ZB, 16), ZB), :]
            for o in (2, 1, 3, 0)[: 4 - turn]:
                i = h * 4 + lax.rem(zh + o, 4)
                far = lax.rem(i + 8 - p, 8)
                copy(wpart.at[blocks_at(i, ZB), :], wz.at[it, p], it, W_RS + far, W_RS + far, dev_p(i)).start()

        ring_wait(*g1_rs)
        total = g1z[it, 0]
        for i in range(1, 8):
            total = total + g1z[it, i]
        g1share[pl.ds(pl.multiple_of(co * (K // 2) + p * 8, 8), 8), :] = total
        share = blocks(g1share.at[half, :], 8)
        g1_ag = (8, p, dev_p, G1_AG, it, lambda i: share(p), share)
        ring(*g1_ag)

        ring_wait(*w_rs)
        total = wz[it, 0]
        for i in range(1, 8):
            total = total + wz[it, i]

        place = blocks(right, ZB)
        w_ag = (8, p, dev_p, W_AG, it, lambda i: place(p), place)
        end_place = blocks(moved, ZB)

        def end_send(i):
            return copy(mine, end_place(p), it, W_AG + i, W_AG + p, (d, i, x * 4 + zl * 2 + co))

        def end_recv(i):
            sender = (d, lax.rem(i, 4) * 2 + yl, x * 4 + lax.div(i, 4) * 2 + co)
            return copy(mine, end_place(i), it, W_AG + i, W_AG + i, sender)

        @pl.when(it < ITERS - 1)
        def _():
            right[blocks_at(p, ZB), :] = total
            ring(*w_ag)

        @pl.when(it == ITERS - 1)
        def _():
            mine[...] = total
            for i in range(8):

                @pl.when((i != z) | (yl != zl))
                def _(i=i):
                    end_send(i).start()

            @pl.when(yl == zl)
            def _():
                moved[blocks_at(p, ZB), :] = total

        ring_wait(*g1_ag)
        swap = copy(g1share.at[half, :], g1share.at[half, :], it, G1_CG, G1_CG, dev_core())
        swap.start()
        swap.wait()
        factor[...] = inverse_factor(g1share[...])

        @pl.when(it < ITERS - 1)
        def _():
            ring_wait(*w_ag)
            right[...] = full_dot(right[...], factor[...], ((1,), (1,)))

        @pl.when(it == ITERS - 1)
        def _():
            for i in range(8):

                @pl.when((i != z) | (yl != zl))
                def _(i=i):
                    end_send(i).wait_send()

                @pl.when((i != p) | (yl != zl))
                def _(i=i):
                    end_recv(i).wait_recv()

            right[...] = full_dot(moved[...], factor[...], ((1,), (1,)))

        rwide[...] = wide(right[...])
        return carry

    lax.fori_loop(0, ITERS, iteration, 0)

    sp = second_plane(ITERS, d * 2 + yl, dev_end_y)
    gram2[...] = full_dot(right[...], right[...], ((0,), (0,)))
    sp.core_copy().start()
    sp.core_done()
    sp.x_send()
    sp.x_done()
    sp.y_send()
    sp.y_done()
    sp.cg_copy().start()
    sp.cg_copy().wait()
    second_out[...] = g2sum[...]
    right_out[...] = right[...]
    out_copy.wait()


def power(partial, start):
    vm = lambda *shape: pltpu.VMEM(shape, F32)
    its = ITERS + 1
    return pl.pallas_call(
        kernel,
        out_shape=(
            jax.ShapeDtypeStruct((TC, K), F32),
            jax.ShapeDtypeStruct((K, K), F32),
            jax.ShapeDtypeStruct((ROWS, HALF), F32),
        ),
        in_specs=[
            pl.BlockSpec(memory_space=pl.ANY),
            pl.BlockSpec(memory_space=pl.ANY),
        ],
        out_specs=[pl.BlockSpec(memory_space=pltpu.VMEM)] * 2 + [pl.BlockSpec(memory_space=pl.ANY)],
        scratch_shapes=[
            vm(ROWS, HALF),
            vm(ROWS, HALF),
            vm(ROWS, HALF),
            vm(TR, TC),
            pltpu.SemaphoreType.DMA((2 * CHUNKS,)),
            pltpu.SemaphoreType.DMA((2 * CHUNKS,)),
            pltpu.SemaphoreType.DMA((CHUNKS,)),
            pltpu.SemaphoreType.DMA,
            pltpu.SemaphoreType.DMA((CHUNKS,)),
            pltpu.SemaphoreType.DMA((CHUNKS,)),
            pltpu.SemaphoreType.DMA((9,)),
            vm(TC, K),
            vm(ZB, K),
            pltpu.VMEM((TR, TC), BF),
            pltpu.VMEM((TR, TC), BF),
            pltpu.VMEM((TC, TR), BF),
            pltpu.VMEM((TC, TR), BF),
            vm(TC, K),
            pltpu.VMEM((TC, 2 * K), BF),
            vm(TR, K),
            vm(TR, K),
            vm(its, TR // 2, K),
            vm(its, 4, TR // 8, K),
            vm(its, 4, TR // 8, K),
            vm(TR, K),
            vm(TC, K),
            vm(its, 8, ZB, K),
            vm(K, K),
            vm(its, 8, 8, K),
            vm(K, K),
            vm(K, K),
            vm(its, K // 2, K),
            vm(its, 4, K // 2, K),
            vm(its, 4, K // 2, K),
            vm(K, K),
            vm(K, K),
            pltpu.SemaphoreType.DMA((its, SEMS)),
            pltpu.SemaphoreType.DMA((its, SEMS)),
        ],
        compiler_params=pltpu.CompilerParams(
            collective_id=0, has_side_effects=True, vmem_limit_bytes=60 * 2**20
        ),
        name="power",
    )(partial, start)


def finish_kernel(summed, right, second, clip_ratio, update_out, basis_out, block, vectors, in_sem, out_sem, right_sem):
    def into(k):
        return pltpu.make_async_copy(summed.at[pl.ds(k * 8, 8), :], block.at[pl.ds(k * 8, 8), :], in_sem.at[k])

    def out(k):
        return pltpu.make_async_copy(block.at[pl.ds(k * 8, 8), :], update_out.at[pl.ds(k * 8, 8), :], out_sem.at[k])

    right_copy = pltpu.make_async_copy(right, vectors, right_sem)
    for k in range(CHUNKS):
        into(k).start()
    right_copy.start()
    sigma = jnp.sqrt(jnp.sqrt(jnp.sum(second[...] * second[...], keepdims=True)))
    scale = clip_ratio[...] * (math.sqrt(M) + math.sqrt(N)) / sigma
    for k in range(CHUNKS):
        into(k).wait()
        block[k * 8 : (k + 1) * 8, :] = block[k * 8 : (k + 1) * 8, :] * scale
        out(k).start()
    factor = inverse_factor(second[...])
    right_copy.wait()
    basis_out[...] = full_dot(vectors[...], factor, ((1,), (1,)))
    for k in range(CHUNKS):
        out(k).wait()


def finish(summed, right, second, clip_ratio):
    return pl.pallas_call(
        finish_kernel,
        out_shape=(jax.ShapeDtypeStruct((ROWS, HALF), F32), jax.ShapeDtypeStruct((TC, K), F32)),
        in_specs=[pl.BlockSpec(memory_space=pl.ANY)] * 2 + [pl.BlockSpec(memory_space=pltpu.VMEM)] * 2,
        out_specs=(pl.BlockSpec(memory_space=pl.ANY), pl.BlockSpec(memory_space=pltpu.VMEM)),
        scratch_shapes=[
            pltpu.VMEM((ROWS, HALF), F32),
            pltpu.VMEM((TC, K), F32),
            pltpu.SemaphoreType.DMA((CHUNKS,)),
            pltpu.SemaphoreType.DMA((CHUNKS,)),
            pltpu.SemaphoreType.DMA,
        ],
        compiler_params=pltpu.CompilerParams(vmem_limit_bytes=60 * 2**20),
        name="finish",
    )(summed, right, second, clip_ratio)


def body(partials, clip_ratio, start_block):
    right, second, summed = power(partials[0], start_block)
    return finish(summed, right, second, clip_ratio.reshape(1, 1))


def solution(mesh):
    placed = (P("dp", ("row", "col"), None), P(), P(("dp", "col"), None))
    return jax.shard_map(
        body,
        mesh=mesh,
        in_specs=placed,
        out_specs=(P(("row", "col"), "dp"), P(("dp", "col"), None)),
        check_vma=False,
    )
```
